32 devices in a mesh: row: 4 (over z), col: 8 (over y, x, core).
Axes of the slice: x: 2, y: 2, z: 4, core: 2. Of those that a mesh axis runs over, the one named last changes fastest.
Arguments:
- tiles: float32 [2, 2304, 4608], P(None, 'row', 'col'), may hold values from -5 to 5
- pupils: float32 [2, 512, 1024], P(None, 'row', 'col'), may hold values from -5 to 5
- intensity: float32 [16, 512, 1024], P(None, 'row', 'col'), may hold values from 0.2 to 3
- offsets: int32 [4, 8, 2, 16], P('row', 'col'), may hold values from 0 to 448
Outputs:
- refocused: float32 [2, 2048, 4096], P(None, 'row', 'col')
The draws below stay inside these ranges and needn't reach their ends.
Inputs may be any that keep to these rules, and one draw needn't show every extreme that they name: `offsets`: each window lies inside the tile's spectrum.
All inputs are finite; a program needn't handle non-finite values.
Results may differ from the reference program's by a relative error of at most 0.00017.
Values sent between devices are 32-bit elements; how exact they have to be, the bound alone decides.
No kernel may reach another device: no remote copies, remote signals or barrier semaphores. Data moves between devices by JAX's collectives and lax.ppermute only.
A program may use at most 128 MiB of HBM per device.

```python
import math
import jax
import jax.numpy as jnp
from jax import lax

TILE = 576
OVL = 64
M = 128
K = 16
STRIDE = 512
NX = 2048
NY = 4096
FRESNEL = 1024
N_ROW = 4
N_COL = 8


def set_ends(drawn, rng, low, largest):
    index_at = [jax.random.randint(jax.random.fold_in(rng, axis), (), 0, length) for axis, length in enumerate(drawn.shape)]
    longest = drawn.shape.index(max(drawn.shape))
    next_to = index_at[:longest] + [(index_at[longest] + 1) % drawn.shape[longest]] + index_at[longest + 1:]
    return drawn.at[tuple(index_at)].set(low).at[tuple(next_to)].set(largest)


def level_of(stream_key, dims, cuts, least, top_value):
    gain, own = 1.0, jax.random.fold_in(stream_key, 6)
    for dim, parts in cuts:
        heights = jnp.exp(jax.random.uniform(jax.random.fold_in(own, dim), (parts,), jnp.float32, least / len(cuts), top_value / len(cuts)))
        gain = gain * jnp.repeat(heights, dims[dim] // parts).reshape([-1 if axis == dim else 1 for axis in range(len(dims))])
    return gain


def scatter_about(key, dims, spread, reach, shards=(), held_as=jnp.bfloat16):
    loudness = level_of(key, dims, shards, -0.22, 0.18) if shards else 1.0
    entries = jax.random.normal(key, dims, jnp.float32) * spread * loudness
    return jnp.minimum(jnp.maximum(entries, -reach), reach).astype(held_as)


def setup_inputs(seed: int = 0) -> dict:
    splits = jax.random.split(jax.random.key(seed), 5)
    return {
        "tiles": scatter_about(splits[0], (2, N_ROW * TILE, N_COL * TILE), 0.7, 5.0, ((1, 4), (2, 8)), jnp.float32),
        "pupils": scatter_about(splits[1], (2, N_ROW * M, N_COL * M), 0.7, 5.0, ((1, 4), (2, 8)), jnp.float32),
        "intensity": jnp.clip(jnp.exp(math.log(3.0) - 2.7080502 * jax.random.uniform(splits[2], (K, N_ROW * M, N_COL * M), jnp.float32) ** level_of(splits[2], (K, N_ROW * M, N_COL * M), ((1, 4), (2, 8)), -0.2, 0.2)), 0.2, 3.0),
        "offsets": set_ends(jax.random.randint(splits[3], (N_ROW, N_COL, 2, K), 0, TILE - M + 1), jax.random.fold_in(splits[3], 1), 0, TILE - M).astype(jnp.int32),
    }


STEP_SIZE = 0.05
TWO_PI = 2.0 * math.pi


def propagator(rows, cols, total_rows, total_cols):
    signed_rows = jnp.where(rows < total_rows // 2, rows, rows - total_rows)
    signed_cols = jnp.where(cols < total_cols // 2, cols, cols - total_cols)
    square_rows = (signed_rows * signed_rows).astype(jnp.float32)
    square_cols = (signed_cols * signed_cols).astype(jnp.float32)
    turns_rows = square_rows * (FRESNEL / (total_rows * total_rows))
    turns_rows = turns_rows - jnp.floor(turns_rows)
    turns_cols = square_cols * (FRESNEL / (total_cols * total_cols))
    turns_cols = turns_cols - jnp.floor(turns_cols)
    angle = (-TWO_PI) * (turns_rows[:, None] + turns_cols[None, :])
    decay = jnp.exp(-2.0 * (square_rows[:, None] / (total_rows * total_rows) + square_cols[None, :] / (total_cols * total_cols)))
    return decay * jnp.cos(angle), decay * jnp.sin(angle)


def refine(item):
    estimate, lens, measured, starts = item
    spectrum = jnp.fft.fft2(estimate, norm="ortho")

    def cut(row_start, col_start):
        return lax.dynamic_slice(spectrum, (row_start, col_start), (M, M))

    crops = jax.vmap(cut)(starts[0], starts[1])
    wave = jnp.fft.ifft2(lens * crops, norm="ortho")
    excess = wave.real * wave.real + wave.imag * wave.imag - measured
    update = jnp.conj(lens) * jnp.fft.fft2(wave * excess, norm="ortho")

    def place(led, total):
        corner = (starts[0, led], starts[1, led])
        current = lax.dynamic_slice(total, corner, (M, M))
        return lax.dynamic_update_slice(total, current + update[led], corner)

    total = lax.fori_loop(0, K, place, jnp.zeros_like(spectrum))
    return jnp.fft.ifft2(spectrum - STEP_SIZE * total, norm="ortho")


def reference(tiles, pupils, intensity, offsets):
    objects = (tiles[0] + 1j * tiles[1]).reshape(N_ROW, TILE, N_COL, TILE).transpose(0, 2, 1, 3).reshape(N_ROW * N_COL, TILE, TILE)
    lenses = (pupils[0] + 1j * pupils[1]).reshape(N_ROW, M, N_COL, M).transpose(0, 2, 1, 3).reshape(N_ROW * N_COL, M, M)
    measured = intensity.reshape(K, N_ROW, M, N_COL, M).transpose(1, 3, 0, 2, 4).reshape(N_ROW * N_COL, K, M, M)
    starts = offsets.reshape(N_ROW * N_COL, 2, K)
    refined = lax.map(refine, (objects, lenses, measured, starts))
    refined = refined.reshape(N_ROW, N_COL, TILE, TILE)
    ramp = (jnp.arange(OVL, dtype=jnp.float32) + 0.5) / OVL
    prior = jnp.roll(refined, 1, axis=0)
    top = ramp[:, None] * refined[:, :, :OVL, :] + (1.0 - ramp)[:, None] * prior[:, :, STRIDE:, :]
    rowed = jnp.concatenate([top, refined[:, :, OVL:STRIDE, :]], axis=2)
    prior = jnp.roll(rowed, 1, axis=1)
    front = ramp * rowed[:, :, :, :OVL] + (1.0 - ramp) * prior[:, :, :, STRIDE:]
    stitched = jnp.concatenate([front, rowed[:, :, :, OVL:STRIDE]], axis=3)
    stitched = stitched.transpose(0, 2, 1, 3).reshape(NX, NY)
    prop_real, prop_imag = propagator(jnp.arange(NX, dtype=jnp.int32), jnp.arange(NY, dtype=jnp.int32), NX, NY)
    result = jnp.fft.ifft2(jnp.fft.fft2(stitched) * (prop_real + 1j * prop_imag))
    return jnp.stack([result.real, result.imag]).astype(jnp.float32)
```

```python
import functools
import math

import jax
import jax.numpy as jnp
import ml_dtypes
import numpy as np
from jax import lax
from jax.experimental import pallas as pl
from jax.experimental.pallas import tpu as pltpu
from jax.sharding import PartitionSpec as P

OVL = 64
STEP_SIZE = 0.05
LANES = 128
RADIX = 4
BF16 = jnp.bfloat16
F32 = jnp.float32


def halves(table):
    table = np.asarray(table, np.float64)
    high = table.astype(np.float32).astype(ml_dtypes.bfloat16)
    low = (table - high.astype(np.float64)).astype(np.float32).astype(ml_dtypes.bfloat16)
    return high, low


def left_block(matrix):
    return np.block([[matrix.real, -matrix.imag], [matrix.imag, matrix.real]])


def right_block(matrix):
    return np.block([[matrix.real, matrix.imag], [-matrix.imag, matrix.real]])


def along_left(block):
    high, low = halves(block)
    return np.concatenate([high, high, low], axis=-1)


def along_right(block):
    high, low = halves(block)
    return np.concatenate([high, high, low], axis=-2)


def dft_matrix(length, sign):
    index = np.arange(length)
    turns = (index[:, None] * index[None, :]) % length
    return np.exp(sign * 2j * np.pi * turns / length) / math.sqrt(length)


def tile_tables(length, sign):
    part = length // RADIX
    index = np.arange(part)
    tables = []
    for residue in range(RADIX):
        turns = (index[None, :] * (residue + RADIX * index[:, None])) % length
        matrix = np.exp(sign * 2j * np.pi * turns / length) / math.sqrt(length)
        tables.append(along_left(left_block(matrix)))
    return np.stack(tables)


def spread_tables(length, fresnel, count, block_of):
    signed = np.arange(length, dtype=np.float64)
    signed = np.where(signed < length // 2, signed, signed - length)
    square = signed * signed
    turns = square * (fresnel / (length * length))
    turns = turns - np.floor(turns)
    kernel = np.fft.ifft(np.exp(-2.0 * square / (length * length)) * np.exp(-2j * np.pi * turns))
    part = length // count
    shift = np.arange(part)[:, None] - np.arange(part)[None, :]
    places = (np.arange(count)[:, None] * part + np.arange(1 - part, part)[None, :]) % length
    classes = np.fft.fft(kernel[places], axis=0) / count
    pairs = [halves(block_of(line[shift + part - 1])) for line in classes]
    return np.stack([pair[0] for pair in pairs]), np.stack([pair[1] for pair in pairs])


def split(value):
    high = value.astype(BF16)
    low = (value - high.astype(F32)).astype(BF16)
    return high, low


def turned(value, eighth_turns, sign):
    real, imag = value
    angle = sign * 2.0 * math.pi * eighth_turns
    if eighth_turns == 0:
        return real, imag
    if eighth_turns == 0.25:
        return (imag, -real) if sign < 0 else (-imag, real)
    cosine, sine = math.cos(angle), math.sin(angle)
    return real * cosine - imag * sine, real * sine + imag * cosine


def short_fft(values, sign):
    count = len(values)
    if count == 1:
        return values
    even = short_fft(values[0::2], sign)
    odd = short_fft(values[1::2], sign)
    low, high = [], []
    for index in range(count // 2):
        real, imag = turned(odd[index], index / count, sign)
        low.append((even[index][0] + real, even[index][1] + imag))
        high.append((even[index][0] - real, even[index][1] - imag))
    return low + high


def tile_pass(source, target, table, operand, sign):
    chunks, length = source.shape[1], source.shape[2]
    part = length // RADIX
    for chunk in range(chunks):
        values = [
            tuple(source[side, chunk, pl.ds(part * step, part), :] for side in range(2))
            for step in range(RADIX)
        ]
        for residue, (real, imag) in enumerate(short_fft(values, sign)):
            lanes = pl.ds(chunk * LANES, LANES)
            for side, value in enumerate((real, imag)):
                high, low = split(value)
                operand[residue, pl.ds(side * part, part), lanes] = high
                operand[residue, pl.ds((2 + side) * part, part), lanes] = low
                operand[residue, pl.ds((4 + side) * part, part), lanes] = high
    for residue in range(RADIX):
        result = jnp.dot(table[residue], operand[residue], preferred_element_type=F32)
        for chunk in range(chunks):
            for side in range(2):
                target[side, chunk, pl.ds(residue, part, stride=RADIX), :] = result[
                    side * part : (side + 1) * part, chunk * LANES : (chunk + 1) * LANES
                ]


def transpose_all(source, target):
    chunks, length = source.shape[1], source.shape[2]
    for side in range(2):
        for chunk in range(chunks):
            rows = min(LANES, length - chunk * LANES)
            for other in range(chunks):
                width = min(LANES, length - other * LANES)
                block = source[side, chunk, pl.ds(other * LANES, width), :]
                target[side, other, pl.ds(chunk * LANES, rows), pl.ds(0, width)] = block.T[:rows]


def refine_kernel(
    starts, tiles, pupils, intensity, to_spectrum, to_object, row_back, col_back, row_fore, col_fore,
    out, first, second, operand, updates,
):
    length = tiles.shape[1]
    window = pupils.shape[1]
    leds = intensity.shape[0]
    chunks = first.shape[1]
    for side in range(2):
        for chunk in range(chunks):
            width = min(LANES, length - chunk * LANES)
            first[side, chunk, :, pl.ds(0, width)] = tiles[side, :, pl.ds(chunk * LANES, width)]
    tile_pass(first, second, to_spectrum, operand, -1)
    transpose_all(second, first)
    tile_pass(first, second, to_spectrum, operand, -1)
    lens_real, lens_imag = pupils[0].T, pupils[1].T
    lane = lax.broadcasted_iota(jnp.int32, (window, LANES), 1)
    group = 8 if leds % 8 == 0 else 1

    def place_of(led):
        start = starts[0, led]
        chunk = start // LANES
        return chunk, start - chunk * LANES, starts[1, led]

    def step(index, carry):
        rows = []
        for member in range(group):
            chunk, shift, row = place_of(index * group + member)
            crop = []
            for side in range(2):
                here = second[side, chunk, pl.ds(row, window), :]
                beyond = second[side, chunk + 1, pl.ds(row, window), :]
                joined = jnp.where(lane >= shift, here, beyond)
                crop.append(pltpu.roll(joined, lax.rem(LANES - shift, LANES), 1))
            rows.append(
                jnp.concatenate(
                    [
                        lens_real * crop[0] - lens_imag * crop[1],
                        lens_real * crop[1] + lens_imag * crop[0],
                    ],
                    axis=1,
                )
            )
        high, low = split(jnp.concatenate(rows, axis=0))
        wave = jnp.dot(
            jnp.concatenate([high, low, high], axis=1), row_back[...], preferred_element_type=F32
        )
        wave = jnp.concatenate(
            [
                jnp.concatenate(
                    [wave[m * window : (m + 1) * window, :window], wave[m * window : (m + 1) * window, window:]],
                    axis=0,
                )
                for m in range(group)
            ],
            axis=1,
        )
        high, low = split(wave)
        wave = jnp.dot(
            col_back[...], jnp.concatenate([high, low, high], axis=0), preferred_element_type=F32
        )
        real, imag = wave[:window], wave[window:]
        measured = jnp.concatenate([intensity[index * group + m].T for m in range(group)], axis=1)
        excess = real * real + imag * imag - measured
        high, low = split(jnp.concatenate([real * excess, imag * excess], axis=0))
        grad = jnp.dot(
            col_fore[...], jnp.concatenate([high, low, high], axis=0), preferred_element_type=F32
        )
        grad = jnp.concatenate(
            [
                jnp.concatenate(
                    [grad[:window, m * window : (m + 1) * window], grad[window:, m * window : (m + 1) * window]],
                    axis=1,
                )
                for m in range(group)
            ],
            axis=0,
        )
        high, low = split(grad)
        grad = jnp.dot(
            jnp.concatenate([high, low, high], axis=1), row_fore[...], preferred_element_type=F32
        )
        for m in range(group):
            real = grad[m * window : (m + 1) * window, :window]
            imag = grad[m * window : (m + 1) * window, window:]
            led = index * group + m
            updates[led, 0] = -STEP_SIZE * (lens_real * real + lens_imag * imag)
            updates[led, 1] = -STEP_SIZE * (lens_real * imag - lens_imag * real)
        return carry

    lax.fori_loop(0, leds // group, step, 0)

    def place(led, carry):
        chunk, shift, row = place_of(led)
        for side in range(2):
            moved = pltpu.roll(updates[led, side], shift, 1)
            second[side, chunk, pl.ds(row, window), :] += jnp.where(lane >= shift, moved, 0.0)
            second[side, chunk + 1, pl.ds(row, window), :] += jnp.where(lane >= shift, 0.0, moved)
        return carry

    lax.fori_loop(0, leds, place, 0)
    tile_pass(second, first, to_object, operand, 1)
    transpose_all(first, second)
    tile_pass(second, first, to_object, operand, 1)
    whole = (length - OVL) // LANES
    count, rows = out.shape[0], out.shape[2]
    for part in range(count):
        have = max(0, min(rows, length - part * rows))
        if have < rows:
            out[part] = jnp.zeros(out.shape[1:], F32)
        if have == 0:
            continue
        here = pl.ds(part * rows, have)
        for side in range(2):
            for chunk in range(whole):
                out[part, side * whole + chunk, pl.ds(0, have), :] = first[side, chunk, here, :]
        halo = first[0, whole, here, :]
        other = pltpu.roll(first[1, whole, here, :], OVL, 1)
        low = lax.broadcasted_iota(jnp.int32, halo.shape, 1) < OVL
        out[part, 2 * whole, pl.ds(0, have), :] = jnp.where(low, halo, other)


def ramp_of(index):
    return (index.astype(F32) + 0.5) / OVL


def col_kernel(values, high_table, low_table, out, held):
    tiles, pieces, rows, _ = values.shape
    whole = (pieces - 1) // 2
    width = out.shape[3] // 2
    per = LANES // width

    def enter(strip, carry):
        here = pl.ds(pl.multiple_of(strip * 8, 8), 8)
        lane = lax.broadcasted_iota(jnp.int32, (8, LANES), 1)
        ramp = jnp.where(lane < OVL, ramp_of(lane), 1.0)
        rest = 1.0 - ramp
        segments = []
        for tile in range(tiles):
            halo = values[(tile - 1) % tiles, 2 * whole, here, :]
            for chunk in range(whole):
                real = values[tile, chunk, here, :]
                imag = values[tile, whole + chunk, here, :]
                if chunk == 0:
                    real = ramp * real + rest * halo
                    imag = ramp * imag + rest * pltpu.roll(halo, OVL, 1)
                segments.append((real, imag))
        for index, (real, imag) in enumerate(short_fft(segments, -1)):
            held[index, here, pl.ds(0, LANES)] = real
            held[index, here, pl.ds(LANES, LANES)] = imag
        return carry

    lax.fori_loop(0, rows // 8, enter, 0)

    def multiply(index, carry):
        value = held[index]
        high = value.astype(BF16)
        both = jnp.concatenate([value, value - high.astype(F32)], axis=0).astype(BF16)
        main = jnp.dot(both, high_table[index], preferred_element_type=F32)
        rest = jnp.dot(high, low_table[index], preferred_element_type=F32)
        held[index] = main[:rows] + (main[rows:] + rest)
        return carry

    lax.fori_loop(0, tiles * whole, multiply, 0)

    def leave(strip, carry):
        here = pl.ds(pl.multiple_of(strip * 8, 8), 8)
        segments = [
            (held[index, here, pl.ds(0, LANES)], held[index, here, pl.ds(LANES, LANES)])
            for index in range(tiles * whole)
        ]
        for index, (real, imag) in enumerate(short_fft(segments, 1)):
            tile, chunk = index // whole, index % whole
            for piece in range(per):
                cut = slice(piece * width, (piece + 1) * width)
                out[chunk * per + piece, tile, here, pl.ds(0, width)] = real[:, cut]
                out[chunk * per + piece, tile, here, pl.ds(width, width)] = imag[:, cut]
        return carry

    lax.fori_loop(0, rows // 8, leave, 0)


def row_kernel(values, high_table, low_table, out, held):
    tiles, _, both = values.shape
    width = both // 2
    stride = out.shape[1]
    part = high_table.shape[1] // 2
    whole = stride // part

    def enter(strip, carry):
        segments = []
        for tile in range(tiles):
            for chunk in range(whole):
                here = pl.ds(pl.multiple_of(chunk * part + strip * 8, 8), 8)
                value = values[tile, here, :]
                if chunk == 0:
                    row = strip * 8 + lax.broadcasted_iota(jnp.int32, (8, both), 0)
                    ramp = jnp.where(row < OVL, ramp_of(row), 1.0)
                    behind = pl.ds(pl.multiple_of(stride + jnp.minimum(strip * 8, OVL - 8), 8), 8)
                    prior = values[(tile - 1) % tiles, behind, :]
                    value = jnp.where(row < OVL, ramp * value + (1.0 - ramp) * prior, value)
                segments.append((value[:, :width], value[:, width:]))
        for index, (real, imag) in enumerate(short_fft(segments, -1)):
            held[index, pl.ds(pl.multiple_of(strip * 8, 8), 8), :] = real
            held[index, pl.ds(pl.multiple_of(part + strip * 8, 8), 8), :] = imag
        return carry

    lax.fori_loop(0, part // 8, enter, 0)

    def multiply(index, carry):
        high, low = split(held[index])
        main = jnp.dot(
            high_table[index], jnp.concatenate([high, low], axis=1), preferred_element_type=F32
        )
        rest = jnp.dot(low_table[index], high, preferred_element_type=F32)
        held[index] = main[:, :width] + (main[:, width:] + rest)
        return carry

    lax.fori_loop(0, tiles * whole, multiply, 0)

    def leave(strip, carry):
        segments = [
            (
                held[index, pl.ds(pl.multiple_of(strip * 8, 8), 8), :],
                held[index, pl.ds(pl.multiple_of(part + strip * 8, 8), 8), :],
            )
            for index in range(tiles * whole)
        ]
        for index, (real, imag) in enumerate(short_fft(segments, 1)):
            tile, chunk = index // whole, index % whole
            here = pl.ds(pl.multiple_of(chunk * part + strip * 8, 8), 8)
            out[tile, here, pl.ds(0, width)] = real
            out[tile, here, pl.ds(width, width)] = imag
        return carry

    lax.fori_loop(0, part // 8, leave, 0)


VMEM = pl.BlockSpec(memory_space=pltpu.VMEM)
SMEM = pl.BlockSpec(memory_space=pltpu.SMEM)


def call(kernel, shape, scratch, limit, *operands, specs=None):
    return pl.pallas_call(
        kernel,
        out_shape=jax.ShapeDtypeStruct(shape, F32),
        in_specs=specs or [VMEM] * len(operands),
        out_specs=VMEM,
        scratch_shapes=scratch,
        compiler_params=pltpu.CompilerParams(vmem_limit_bytes=limit << 20),
    )(*operands)


def local(row_count, col_count, tiles, pupils, intensity, offsets):
    length = tiles.shape[1]
    window = pupils.shape[1]
    leds = intensity.shape[0]
    stride = length - OVL
    whole = stride // LANES
    chunks = whole + 1
    rows = -(-length // (8 * col_count)) * 8
    width = stride // row_count
    fresnel = stride * row_count // 2
    fore, back = dft_matrix(window, -1), dft_matrix(window, 1)
    part = length // RADIX
    field = call(
        refine_kernel,
        (col_count, 2 * whole + 1, rows, LANES),
        [
            pltpu.VMEM((2, chunks, length, LANES), F32),
            pltpu.VMEM((2, chunks, length, LANES), F32),
            pltpu.VMEM((RADIX, 6 * part, chunks * LANES), BF16),
            pltpu.VMEM((leds, 2, window, window), F32),
        ],
        56,
        offsets[0, 0],
        tiles,
        pupils,
        intensity,
        tile_tables(length, -1),
        tile_tables(length, 1),
        along_right(right_block(back)),
        along_left(left_block(back)),
        along_right(right_block(fore)),
        along_left(left_block(fore)),
        specs=[SMEM] + [VMEM] * 9,
    )
    field = lax.all_to_all(field, "col", split_axis=0, concat_axis=0, tiled=True)
    col_classes = col_count * whole
    field = call(
        col_kernel,
        (row_count, col_count, rows, 2 * width),
        [pltpu.VMEM((col_classes, rows, 2 * LANES), F32)],
        40,
        field,
        *spread_tables(stride * col_count, fresnel, col_classes, lambda m: right_block(m.T)),
    )
    field = lax.all_to_all(
        field.reshape(row_count * col_count, rows, 2 * width),
        ("row", "col"),
        split_axis=0,
        concat_axis=0,
        tiled=True,
    )
    row_classes = row_count * whole
    field = call(
        row_kernel,
        (row_count, stride, 2 * width),
        [pltpu.VMEM((row_classes, 2 * LANES, width), F32)],
        40,
        field.reshape(row_count, col_count * rows, 2 * width),
        *spread_tables(stride * row_count, fresnel, row_classes, left_block),
    )
    field = lax.all_to_all(field, "row", split_axis=0, concat_axis=0, tiled=True)
    field = field.reshape(row_count, stride, 2, width).transpose(2, 1, 0, 3)
    return field.reshape(2, stride, stride)


def solution(mesh):
    placed = (
        P(None, "row", "col"),
        P(None, "row", "col"),
        P(None, "row", "col"),
        P("row", "col", None, None),
    )
    return jax.shard_map(
        functools.partial(local, mesh.shape["row"], mesh.shape["col"]),
        mesh=mesh,
        in_specs=placed,
        out_specs=P(None, "row", "col"),
        check_vma=False,
    )
```

```python
import functools
import math

import jax
import jax.numpy as jnp
import ml_dtypes
import numpy as np
from jax import lax
from jax.experimental import pallas as pl
from jax.experimental.pallas import tpu as pltpu
from jax.sharding import PartitionSpec as P

OVL = 64
STEP_SIZE = 0.05
LANES = 128
RADIX = 8
BF16 = jnp.bfloat16
F32 = jnp.float32


def halves(table):
    table = np.asarray(table, np.float64)
    high = table.astype(np.float32).astype(ml_dtypes.bfloat16)
    low = (table - high.astype(np.float64)).astype(np.float32).astype(ml_dtypes.bfloat16)
    return high, low


def left_half(matrix):
    return np.concatenate([matrix.real, matrix.imag], axis=0)


def right_half(matrix):
    return np.concatenate([matrix.real, matrix.imag], axis=1)


def left_block(matrix):
    return np.block([[matrix.real, -matrix.imag], [matrix.imag, matrix.real]])


def right_block(matrix):
    return np.block([[matrix.real, matrix.imag], [-matrix.imag, matrix.real]])


def along_left(block):
    high, low = halves(block)
    return np.concatenate([high, high, low], axis=-1)


def along_right(block):
    high, low = halves(block)
    return np.concatenate([high, high, low], axis=-2)


def dft_matrix(length):
    index = np.arange(length)
    turns = (index[:, None] * index[None, :]) % length
    return np.exp(-2j * np.pi * turns / length) / math.sqrt(length)


def tile_tables(length):
    part = length // RADIX
    index = np.arange(part)
    tables = []
    for residue in range(RADIX):
        turns = (index[None, :] * (residue + RADIX * index[:, None])) % length
        matrix = np.exp(-2j * np.pi * turns / length) / math.sqrt(length)
        tables.append(along_left(left_half(matrix)))
    return np.stack(tables)


def spread_tables(length, fresnel, count, block_of):
    signed = np.arange(length, dtype=np.float64)
    signed = np.where(signed < length // 2, signed, signed - length)
    square = signed * signed
    turns = square * (fresnel / (length * length))
    turns = turns - np.floor(turns)
    kernel = np.fft.ifft(np.exp(-2.0 * square / (length * length)) * np.exp(-2j * np.pi * turns))
    part = length // count
    shift = np.arange(part)[:, None] - np.arange(part)[None, :]
    places = (np.arange(count)[:, None] * part + np.arange(1 - part, part)[None, :]) % length
    classes = np.fft.fft(kernel[places], axis=0) / count
    pairs = [halves(block_of(line[shift + part - 1])) for line in classes]
    return np.stack([np.stack([pair[0] for pair in pairs]), np.stack([pair[1] for pair in pairs])])


def split(value):
    high = value.astype(BF16)
    low = (value - high.astype(F32)).astype(BF16)
    return high, low


def turned(value, eighth_turns, sign):
    real, imag = value
    angle = sign * 2.0 * math.pi * eighth_turns
    if eighth_turns == 0:
        return real, imag
    if eighth_turns == 0.25:
        return (imag, -real) if sign < 0 else (-imag, real)
    cosine, sine = math.cos(angle), math.sin(angle)
    return real * cosine - imag * sine, real * sine + imag * cosine


def short_fft(values, sign):
    count = len(values)
    if count == 1:
        return values
    even = short_fft(values[0::2], sign)
    odd = short_fft(values[1::2], sign)
    low, high = [], []
    for index in range(count // 2):
        real, imag = turned(odd[index], index / count, sign)
        low.append((even[index][0] + real, even[index][1] + imag))
        high.append((even[index][0] - real, even[index][1] - imag))
    return low + high


def tile_pass(load, target, table, sign):
    part = table.shape[1] // 2
    for chunk in range(target.shape[1]):
        values = [
            tuple(load(side, chunk, pl.ds(part * step, part)) for side in range(2))
            for step in range(RADIX)
        ]
        for residue, value in enumerate(short_fft(values, sign)):
            value = jnp.concatenate(value, axis=1)
            high = value.astype(BF16).astype(F32)
            stacked = jnp.concatenate([high, value - high, high], axis=0).astype(BF16)
            result = jnp.dot(table[residue], stacked, preferred_element_type=F32)
            plain, crossed = result[:part], result[part:]
            real, imag = plain[:, :LANES], plain[:, LANES:]
            if sign < 0:
                real, imag = real - crossed[:, LANES:], imag + crossed[:, :LANES]
            else:
                real, imag = real + crossed[:, LANES:], imag - crossed[:, :LANES]
            rows = pl.ds(residue, part, stride=RADIX)
            target[0, chunk, rows, :] = real
            target[1, chunk, rows, :] = imag


def transpose_all(source, target):
    chunks, length = source.shape[1], source.shape[2]
    for side in range(2):
        for chunk in range(chunks):
            rows = min(LANES, length - chunk * LANES)
            for other in range(chunks):
                width = min(LANES, length - other * LANES)
                block = source[side, chunk, pl.ds(other * LANES, width), :]
                target[side, other, pl.ds(chunk * LANES, rows), pl.ds(0, width)] = block.T[:rows]


def refine_kernel(starts, *refs):
    sources, (late, early, below), refs = refs[:6], refs[6:9], refs[9:]
    held, (first, second, updates, done) = refs[:6], refs[6:]
    tiles, table, pupils, intensity, row_table, col_table = held
    copies = [
        pltpu.make_async_copy(source, target, done.at[place])
        for place, (source, target) in enumerate(zip(sources, held))
    ]
    for copy in copies:
        copy.start()
    length = tiles.shape[1]
    window = pupils.shape[1]
    leds = intensity.shape[0]
    chunks = first.shape[1]
    rest = length - (chunks - 1) * LANES
    copies[0].wait()
    for side in range(2):
        second[side, chunks - 1, :, pl.ds(0, rest)] = tiles[side, :, pl.ds((chunks - 1) * LANES, rest)]

    def from_tiles(side, chunk, rows):
        if chunk == chunks - 1:
            return second[side, chunk, rows, :]
        return tiles[side, rows, pl.ds(chunk * LANES, LANES)]

    def from_first(side, chunk, rows):
        return first[side, chunk, rows, :]

    def from_second(side, chunk, rows):
        return second[side, chunk, rows, :]

    copies[1].wait()
    tile_pass(from_tiles, first, table, -1)
    transpose_all(first, second)
    tile_pass(from_second, first, table, -1)
    for copy in copies[2:]:
        copy.wait()
    lens_real, lens_imag = pupils[0].T, pupils[1].T
    lane = lax.broadcasted_iota(jnp.int32, (window, LANES), 1)
    group = 8 if leds % 8 == 0 else 1

    def place_of(led):
        start = starts[0, led]
        chunk = start // LANES
        return chunk, start - chunk * LANES, starts[1, led]

    def along_rows(value):
        high, low = split(value)
        return jnp.dot(
            jnp.concatenate([high, low, high], axis=1), row_table[...], preferred_element_type=F32
        )

    def along_cols(value):
        high, low = split(value)
        return jnp.dot(
            col_table[...], jnp.concatenate([high, low, high], axis=0), preferred_element_type=F32
        )

    def step(index, carry):
        crops = []
        for member in range(group):
            chunk, shift, row = place_of(index * group + member)
            crop = []
            for side in range(2):
                here = first[side, chunk, pl.ds(row, window), :]
                beyond = first[side, chunk + 1, pl.ds(row, window), :]
                joined = jnp.where(lane >= shift, here, beyond)
                crop.append(pltpu.roll(joined, lax.rem(LANES - shift, LANES), 1))
            crops.append(
                jnp.concatenate(
                    [
                        lens_real * crop[0] - lens_imag * crop[1],
                        -lens_real * crop[1] - lens_imag * crop[0],
                    ],
                    axis=1,
                )
            )
        wave = along_rows(jnp.concatenate(crops, axis=0))
        blocks = [wave[m * window : (m + 1) * window] for m in range(group)]
        blocks = [jnp.concatenate([b[:, :window], b[:, window:]], axis=0) for b in blocks]
        wave = along_cols(jnp.concatenate(blocks, axis=1))
        real, imag = wave[:window], wave[window:]
        measured = jnp.concatenate([intensity[index * group + m].T for m in range(group)], axis=1)
        excess = real * real + imag * imag - measured
        grad = along_cols(jnp.concatenate([real * excess, -imag * excess], axis=0))
        blocks = [grad[:, m * window : (m + 1) * window] for m in range(group)]
        blocks = [jnp.concatenate([b[:window], b[window:]], axis=1) for b in blocks]
        grad = along_rows(jnp.concatenate(blocks, axis=0))
        for m in range(group):
            real = grad[m * window : (m + 1) * window, :window]
            imag = grad[m * window : (m + 1) * window, window:]
            led = index * group + m
            updates[led, 0] = -STEP_SIZE * (lens_real * real + lens_imag * imag)
            updates[led, 1] = -STEP_SIZE * (lens_real * imag - lens_imag * real)
        return carry

    lax.fori_loop(0, leds // group, step, 0)

    def place(led, carry):
        chunk, shift, row = place_of(led)
        for side in range(2):
            moved = pltpu.roll(updates[led, side], shift, 1)
            first[side, chunk, pl.ds(row, window), :] += jnp.where(lane >= shift, moved, 0.0)
            first[side, chunk + 1, pl.ds(row, window), :] += jnp.where(lane >= shift, 0.0, moved)
        return carry

    lax.fori_loop(0, leds, place, 0, unroll=4)
    tile_pass(from_first, second, table, 1)
    transpose_all(second, first)
    tile_pass(from_first, second, table, 1)
    whole = (length - OVL) // LANES
    count, _, rows, _ = late.shape

    def emit(target, part, row, gain):
        here = pl.ds(row, rows)
        for side in range(2):
            for chunk in range(whole):
                target[part, side * whole + chunk] = scaled(second[side, chunk, here, :], gain)
        near = second[0, whole, here, :]
        far = pltpu.roll(second[1, whole, here, :], OVL, 1)
        low = lax.broadcasted_iota(jnp.int32, near.shape, 1) < OVL
        target[part, 2 * whole] = scaled(jnp.where(low, near, far), gain)

    for part in range(count):
        segment, offset = divmod(part * rows, OVL)
        emit(late, part, segment * LANES + OVL + offset, None)
        ramp = None
        if segment == 0:
            ramp = ramp_of(offset + lax.broadcasted_iota(jnp.int32, (rows, LANES), 0))
            emit(below, part, whole * LANES + offset, 1.0 - ramp)
        emit(early, part, segment * LANES + offset, ramp)


def scaled(value, gain):
    return value if gain is None else value * gain


def ramp_of(index):
    return (index.astype(F32) + 0.5) / OVL


def spread_kernel(place, early, above, *outs):
    blended = above.shape[0]
    for step, out in enumerate(outs):
        part = jnp.bitwise_xor(place[0], step)
        out[...] = early[part]

        @pl.when(part < blended)
        def _():
            out[...] += above[jnp.minimum(part, blended - 1)]


UNROLL = 4


class Fetch:
    def __init__(self, source, target, done):
        self.parts = done.shape[0]
        self.each = source.shape[1] // self.parts
        self.copies = [
            pltpu.make_async_copy(
                source.at[:, pl.ds(part * self.each, self.each)],
                target.at[:, pl.ds(part * self.each, self.each)],
                done.at[part],
            )
            for part in range(self.parts)
        ]
        for copy in self.copies:
            copy.start()

    def each_class(self, body):
        for part in range(self.parts):
            self.copies[part].wait()
            lax.fori_loop(part * self.each, (part + 1) * self.each, body, 0, unroll=UNROLL)


def col_kernel(place, late, *refs):
    *blocks, table_source, out, early, held, table, done = refs
    fetch = Fetch(table_source, table, done)
    for step, block in enumerate(blocks):
        early[jnp.bitwise_xor(place[0], step)] = block[...]
    tiles, pieces, half, _ = late.shape
    rows = 2 * half
    whole = (pieces - 1) // 2
    width = out.shape[3] // 2
    per = LANES // width

    def enter_from(values, first):
        def enter(strip, carry):
            here = pl.ds(pl.multiple_of(strip * 8, 8), 8)
            lane = lax.broadcasted_iota(jnp.int32, (8, LANES), 1)
            ramp = jnp.where(lane < OVL, ramp_of(lane), 1.0)
            rest = 1.0 - ramp
            segments = []
            for tile in range(tiles):
                halo = values[(tile - 1) % tiles, 2 * whole, here, :]
                for chunk in range(whole):
                    real = values[tile, chunk, here, :]
                    imag = values[tile, whole + chunk, here, :]
                    if chunk == 0:
                        real = ramp * real + rest * halo
                        imag = ramp * imag + rest * pltpu.roll(halo, OVL, 1)
                    segments.append((real, imag))
            here = pl.ds(pl.multiple_of(first + strip * 8, 8), 8)
            for index, (real, imag) in enumerate(short_fft(segments, -1)):
                held[index, 0, here, :] = real
                held[index, 1, here, :] = imag
            return carry

        lax.fori_loop(0, half // 8, enter, 0)

    enter_from(late, 0)
    enter_from(early, half)

    def multiply(index, carry):
        value = held[index].reshape(2 * rows, LANES)
        high = value.astype(BF16)
        both = jnp.concatenate([value, value - high.astype(F32)], axis=0).astype(BF16)
        main = jnp.dot(both, table[0, index], preferred_element_type=F32)
        rest = jnp.dot(high, table[1, index], preferred_element_type=F32)
        full = main[: 2 * rows] + (main[2 * rows :] + rest)
        held[index, 0] = full[:rows, :LANES] - full[rows:, LANES:]
        held[index, 1] = full[:rows, LANES:] + full[rows:, :LANES]
        return carry

    fetch.each_class(multiply)

    def leave(strip, carry):
        here = pl.ds(pl.multiple_of(strip * 8, 8), 8)
        segments = [
            (held[index, 0, here, :], held[index, 1, here, :]) for index in range(tiles * whole)
        ]
        for index, (real, imag) in enumerate(short_fft(segments, 1)):
            tile, chunk = index // whole, index % whole
            for piece in range(per):
                cut = slice(piece * width, (piece + 1) * width)
                out[chunk * per + piece, tile, here, pl.ds(0, width)] = real[:, cut]
                out[chunk * per + piece, tile, here, pl.ds(width, width)] = imag[:, cut]
        return carry

    lax.fori_loop(0, rows // 8, leave, 0)


def row_kernel(half, place, values, table_source, *refs):
    *outs, out, held, table, done = refs
    fetch = Fetch(table_source, table, done)
    tiles, _, both = values.shape
    width = both // 2
    stride = out.shape[1]
    part = table.shape[3]
    whole = stride // part

    def enter_from(offset, first):
        def enter(strip, carry):
            segments = []
            for tile in range(tiles):
                for chunk in range(whole):
                    row = chunk * OVL + strip * 8
                    row = row // half * (2 * half) + lax.rem(row, half) + offset
                    value = values[tile, pl.ds(pl.multiple_of(row, 8), 8), :]
                    segments.append((value[:, :width], value[:, width:]))
            here = pl.ds(pl.multiple_of(first + strip * 8, 8), 8)
            for index, (real, imag) in enumerate(short_fft(segments, -1)):
                held[index, here, pl.ds(0, width)] = real
                held[index, here, pl.ds(width, width)] = imag
            return carry

        lax.fori_loop(0, OVL // 8, enter, 0)

    enter_from(half, 0)
    enter_from(0, OVL)

    def multiply(index, carry):
        high, low = split(held[index])
        main = jnp.dot(
            table[0, index], jnp.concatenate([high, low], axis=1), preferred_element_type=F32
        )
        rest = jnp.dot(table[1, index], high, preferred_element_type=F32)
        full = main[:, :both] + (main[:, both:] + rest)
        held[index, :, pl.ds(0, width)] = full[:part, :width] - full[part:, width:]
        held[index, :, pl.ds(width, width)] = full[:part, width:] + full[part:, :width]
        return carry

    fetch.each_class(multiply)

    def leave(strip, carry):
        here = pl.ds(pl.multiple_of(strip * 8, 8), 8)
        segments = []
        for index in range(tiles * whole):
            value = held[index, here, :]
            segments.append((value[:, :width], value[:, width:]))
        for index, (real, imag) in enumerate(short_fft(segments, 1)):
            tile, chunk = index // whole, index % whole
            here = pl.ds(pl.multiple_of(chunk * part + strip * 8, 8), 8)
            out[tile, here, pl.ds(0, width)] = real
            out[tile, here, pl.ds(width, width)] = imag
        return carry

    lax.fori_loop(0, part // 8, leave, 0)
    for step, target in enumerate(outs):
        target[...] = out[jnp.bitwise_xor(place[1], step)]


def join_kernel(place, *refs):
    *blocks, out, ordered = refs
    count, _, both = ordered.shape
    width = both // 2
    for step, block in enumerate(blocks):
        part = jnp.bitwise_xor(place[1], step)
        if width % LANES:
            ordered[part] = block[...]
            continue
        for side in range(2):
            lanes = pl.ds(pl.multiple_of(part * width, LANES), width)
            out[side, :, lanes] = block[:, pl.ds(side * width, width)]
    if width % LANES:
        for part in range(count):
            for side in range(2):
                out[side, :, pl.ds(part * width, width)] = ordered[part, :, pl.ds(side * width, width)]


VMEM = pl.BlockSpec(memory_space=pltpu.VMEM)
SMEM = pl.BlockSpec(memory_space=pltpu.SMEM)
HBM = pl.BlockSpec(memory_space=pltpu.HBM)


def call(kernel, shapes, scratch, limit, micros, *operands, scalars=0, outside=()):
    return pl.pallas_call(
        kernel,
        out_shape=[jax.ShapeDtypeStruct(shape, F32) for shape in shapes],
        in_specs=[
            SMEM if place < scalars else HBM if place - len(operands) in outside else VMEM
            for place in range(len(operands))
        ],
        out_specs=[VMEM] * len(shapes),
        scratch_shapes=scratch,
        cost_estimate=pl.CostEstimate(
            flops=int(micros * 5e8), bytes_accessed=int(micros * 2e6), transcendentals=0
        ),
        compiler_params=pltpu.CompilerParams(vmem_limit_bytes=limit << 20),
    )(*operands)


def local(row_count, col_count, tiles, pupils, intensity, offsets):
    length = tiles.shape[1]
    window = pupils.shape[1]
    leds = intensity.shape[0]
    stride = length - OVL
    whole = stride // LANES
    chunks = whole + 1
    rows = stride // (2 * col_count)
    width = stride // row_count
    fresnel = stride * row_count // 2
    block = (2 * whole + 1, rows, LANES)
    operands = (
        tiles,
        tile_tables(length),
        pupils,
        intensity,
        along_right(right_block(dft_matrix(window))),
        along_left(left_block(dft_matrix(window))),
    )
    buffer = pltpu.VMEM((2, chunks, length, LANES), F32)
    late, early, below = call(
        refine_kernel,
        [(col_count, *block), (col_count, *block), (OVL // rows, *block)],
        [pltpu.VMEM(operand.shape, operand.dtype) for operand in operands]
        + [
            buffer,
            buffer,
            pltpu.VMEM((leds, 2, window, window), F32),
            pltpu.SemaphoreType.DMA((len(operands),)),
        ],
        56,
        22,
        offsets[0, 0],
        *operands,
        scalars=1,
        outside=range(-len(operands), 0),
    )
    above = lax.ppermute(below, "row", [(r, (r + 1) % row_count) for r in range(row_count)])
    late = lax.all_to_all(late, "col", split_axis=0, concat_axis=0, tiled=True)
    place = jnp.stack([lax.axis_index("col"), lax.axis_index("row")]).astype(jnp.int32)
    early = call(spread_kernel, [block] * col_count, [], 16, 1, place, early, above, scalars=1)
    early = [early[0]] + [
        lax.ppermute(early[step], "col", [(c, c ^ step) for c in range(col_count)])
        for step in range(1, col_count)
    ]
    col_classes = col_count * whole
    table = spread_tables(stride * col_count, fresnel, col_classes, lambda m: right_half(m.T))
    (field,) = call(
        col_kernel,
        [(row_count, col_count, 2 * rows, 2 * width)],
        [
            pltpu.VMEM((col_count, *block), F32),
            pltpu.VMEM((col_classes, 2, 2 * rows, LANES), F32),
            pltpu.VMEM(table.shape, BF16),
            pltpu.SemaphoreType.DMA((4,)),
        ],
        32,
        5,
        place,
        late,
        *early,
        table,
        scalars=1,
        outside=(-1,),
    )
    field = field.reshape(row_count * col_count, 2 * rows, 2 * width)
    field = lax.all_to_all(field, ("row", "col"), split_axis=0, concat_axis=0, tiled=True)
    row_classes = row_count * whole
    table = spread_tables(stride * row_count, fresnel, row_classes, left_half)
    shape = (stride, 2 * width)
    blocks = call(
        functools.partial(row_kernel, rows),
        [shape] * row_count,
        [
            pltpu.VMEM((row_count, *shape), F32),
            pltpu.VMEM((row_classes, LANES, 2 * width), F32),
            pltpu.VMEM(table.shape, BF16),
            pltpu.SemaphoreType.DMA((4,)),
        ],
        32,
        5,
        place,
        field.reshape(row_count, col_count * 2 * rows, 2 * width),
        table,
        scalars=1,
        outside=(-1,),
    )
    blocks = [blocks[0]] + [
        lax.ppermute(blocks[step], "row", [(r, r ^ step) for r in range(row_count)])
        for step in range(1, row_count)
    ]
    (field,) = call(
        join_kernel,
        [(2, stride, stride)],
        [pltpu.VMEM((row_count, *shape), F32)],
        16,
        2,
        place,
        *blocks,
        scalars=1,
    )
    return field


def solution(mesh):
    placed = (
        P(None, "row", "col"),
        P(None, "row", "col"),
        P(None, "row", "col"),
        P("row", "col", None, None),
    )
    return jax.shard_map(
        functools.partial(local, mesh.shape["row"], mesh.shape["col"]),
        mesh=mesh,
        in_specs=placed,
        out_specs=P(None, "row", "col"),
        check_vma=False,
    )
```

```python
import functools
import math

import jax
import jax.numpy as jnp
import ml_dtypes
import numpy as np
from jax import lax
from jax.experimental import pallas as pl
from jax.experimental.pallas import tpu as pltpu
from jax.sharding import PartitionSpec as P

OVL = 64
STEP_SIZE = 0.05
LANES = 128
RADIX = 8
BF16 = jnp.bfloat16
F32 = jnp.float32


def halves(table):
    table = np.asarray(table, np.float64)
    high = table.astype(np.float32).astype(ml_dtypes.bfloat16)
    low = (table - high.astype(np.float64)).astype(np.float32).astype(ml_dtypes.bfloat16)
    return high, low


def left_half(matrix):
    return np.concatenate([matrix.real, matrix.imag], axis=0)


def right_half(matrix):
    return np.concatenate([matrix.real, matrix.imag], axis=1)


def left_block(matrix):
    return np.block([[matrix.real, -matrix.imag], [matrix.imag, matrix.real]])


def right_block(matrix):
    return np.block([[matrix.real, matrix.imag], [-matrix.imag, matrix.real]])


def along_left(block):
    high, low = halves(block)
    return np.concatenate([high, high, low], axis=-1)


def along_right(block):
    high, low = halves(block)
    return np.concatenate([high, high, low], axis=-2)


def dft_matrix(length):
    index = np.arange(length)
    turns = (index[:, None] * index[None, :]) % length
    return np.exp(-2j * np.pi * turns / length) / math.sqrt(length)


def tile_tables(length):
    part = length // RADIX
    index = np.arange(part)
    tables = []
    for residue in range(RADIX):
        turns = (index[None, :] * (residue + RADIX * index[:, None])) % length
        matrix = np.exp(-2j * np.pi * turns / length) / math.sqrt(length)
        tables.append(along_left(left_half(matrix)))
    return np.stack(tables)


def spread_tables(length, fresnel, count, block_of):
    signed = np.arange(length, dtype=np.float64)
    signed = np.where(signed < length // 2, signed, signed - length)
    square = signed * signed
    turns = square * (fresnel / (length * length))
    turns = turns - np.floor(turns)
    kernel = np.fft.ifft(np.exp(-2.0 * square / (length * length)) * np.exp(-2j * np.pi * turns))
    part = length // count
    shift = np.arange(part)[:, None] - np.arange(part)[None, :]
    places = (np.arange(count)[:, None] * part + np.arange(1 - part, part)[None, :]) % length
    classes = np.fft.fft(kernel[places], axis=0) / count
    pairs = [halves(block_of(line[shift + part - 1])) for line in classes]
    return np.stack([np.stack([pair[0] for pair in pairs]), np.stack([pair[1] for pair in pairs])])


def split(value):
    high = value.astype(BF16)
    low = (value - high.astype(F32)).astype(BF16)
    return high, low


def turned(value, eighth_turns, sign):
    real, imag = value
    angle = sign * 2.0 * math.pi * eighth_turns
    if eighth_turns == 0:
        return real, imag
    if eighth_turns == 0.25:
        return (imag, -real) if sign < 0 else (-imag, real)
    cosine, sine = math.cos(angle), math.sin(angle)
    return real * cosine - imag * sine, real * sine + imag * cosine


def short_fft(values, sign):
    count = len(values)
    if count == 1:
        return values
    even = short_fft(values[0::2], sign)
    odd = short_fft(values[1::2], sign)
    low, high = [], []
    for index in range(count // 2):
        real, imag = turned(odd[index], index / count, sign)
        low.append((even[index][0] + real, even[index][1] + imag))
        high.append((even[index][0] - real, even[index][1] - imag))
    return low + high


def tile_pass(load, target, table, sign):
    part = table.shape[1] // 2
    for chunk in range(target.shape[1]):
        values = [
            tuple(load(side, chunk, pl.ds(part * step, part)) for side in range(2))
            for step in range(RADIX)
        ]
        for residue, value in enumerate(short_fft(values, sign)):
            value = jnp.concatenate(value, axis=1)
            high = value.astype(BF16).astype(F32)
            stacked = jnp.concatenate([high, value - high, high], axis=0).astype(BF16)
            result = jnp.dot(table[residue], stacked, preferred_element_type=F32)
            plain, crossed = result[:part], result[part:]
            real, imag = plain[:, :LANES], plain[:, LANES:]
            if sign < 0:
                real, imag = real - crossed[:, LANES:], imag + crossed[:, :LANES]
            else:
                real, imag = real + crossed[:, LANES:], imag - crossed[:, :LANES]
            rows = pl.ds(residue, part, stride=RADIX)
            target[0, chunk, rows, :] = real
            target[1, chunk, rows, :] = imag


def transpose_all(source, target):
    chunks, length = source.shape[1], source.shape[2]
    for side in range(2):
        for chunk in range(chunks):
            rows = min(LANES, length - chunk * LANES)
            for other in range(chunks):
                width = min(LANES, length - other * LANES)
                block = source[side, chunk, pl.ds(other * LANES, width), :]
                target[side, other, pl.ds(chunk * LANES, rows), pl.ds(0, width)] = block.T[:rows]


def refine_kernel(starts, *refs):
    sources, (late, early, below), refs = refs[:6], refs[6:9], refs[9:]
    held, (first, second, updates, arrived, done) = refs[:6], refs[6:]
    tiles, table, pupils, intensity, row_table, col_table = held
    length = tiles.shape[1]
    window = pupils.shape[1]
    leds = intensity.shape[0]
    chunks = first.shape[1]
    rest = length - (chunks - 1) * LANES
    tile_copies = []
    for chunk in range(chunks):
        lanes = pl.ds(chunk * LANES, min(LANES, length - chunk * LANES))
        tile_copies.append(
            pltpu.make_async_copy(sources[0].at[:, :, lanes], tiles.at[:, :, lanes], arrived.at[chunk])
        )
    copies = [
        pltpu.make_async_copy(source, target, done.at[place])
        for place, (source, target) in enumerate(zip(sources[1:], held[1:]))
    ]
    tile_copies[0].start()
    copies[0].start()
    for copy in tile_copies[1:] + copies[1:]:
        copy.start()

    def from_tiles(side, chunk, rows):
        if side == 0 and rows.start == 0:
            tile_copies[chunk].wait()
            if chunk == chunks - 1:
                for part in range(2):
                    second[part, chunk, :, pl.ds(0, rest)] = tiles[part, :, pl.ds(chunk * LANES, rest)]
        if chunk == chunks - 1:
            return second[side, chunk, rows, :]
        return tiles[side, rows, pl.ds(chunk * LANES, LANES)]

    def from_first(side, chunk, rows):
        return first[side, chunk, rows, :]

    def from_second(side, chunk, rows):
        return second[side, chunk, rows, :]

    copies[0].wait()
    tile_pass(from_tiles, first, table, -1)
    transpose_all(first, second)
    tile_pass(from_second, first, table, -1)
    for copy in copies[1:]:
        copy.wait()
    lens_real, lens_imag = pupils[0].T, pupils[1].T
    lane = lax.broadcasted_iota(jnp.int32, (window, LANES), 1)
    group, beside = (GROUP, BESIDE) if leds % (GROUP * BESIDE) == 0 else (1, 1)

    def place_of(led):
        start = starts[0, led]
        chunk = start // LANES
        return chunk, start - chunk * LANES, starts[1, led]

    def along_rows(value):
        high, low = split(value)
        return jnp.dot(
            jnp.concatenate([high, low, high], axis=1), row_table[...], preferred_element_type=F32
        )

    def along_cols(value):
        high, low = split(value)
        return jnp.dot(
            col_table[...], jnp.concatenate([high, low, high], axis=0), preferred_element_type=F32
        )

    def crop(led):
        chunk, shift, row = place_of(led)
        crop = []
        for side in range(2):
            here = first[side, chunk, pl.ds(row, window), :]
            beyond = first[side, chunk + 1, pl.ds(row, window), :]
            joined = jnp.where(lane >= shift, here, beyond)
            crop.append(pltpu.roll(joined, lax.rem(LANES - shift, LANES), 1))
        real = lens_real * crop[0] - lens_imag * crop[1]
        imag = -lens_real * crop[1] - lens_imag * crop[0]
        return jnp.concatenate([real, imag], axis=1)

    def to_waves(leds):
        return along_rows(jnp.concatenate([crop(led) for led in leds], axis=0))

    def to_wave_cols(leds, wave):
        blocks = [wave[m * window : (m + 1) * window] for m in range(len(leds))]
        blocks = [jnp.concatenate([b[:, :window], b[:, window:]], axis=0) for b in blocks]
        return along_cols(jnp.concatenate(blocks, axis=1))

    def to_grad_cols(leds, wave):
        real, imag = wave[:window], wave[window:]
        measured = jnp.concatenate([intensity[led].T for led in leds], axis=1)
        excess = real * real + imag * imag - measured
        return along_cols(jnp.concatenate([real * excess, -imag * excess], axis=0))

    def to_grads(leds, grad):
        blocks = [grad[:, m * window : (m + 1) * window] for m in range(len(leds))]
        blocks = [jnp.concatenate([b[:window], b[window:]], axis=1) for b in blocks]
        return along_rows(jnp.concatenate(blocks, axis=0))

    def to_updates(leds, grad):
        for m, led in enumerate(leds):
            real = grad[m * window : (m + 1) * window, :window]
            imag = grad[m * window : (m + 1) * window, window:]
            updates[led, 0] = -STEP_SIZE * (lens_real * real + lens_imag * imag)
            updates[led, 1] = -STEP_SIZE * (lens_real * imag - lens_imag * real)

    def step(index, carry):
        groups = [
            [(index * beside + g) * group + m for m in range(group)] for g in range(beside)
        ]
        values = [to_waves(g) for g in groups]
        for stage in (to_wave_cols, to_grad_cols, to_grads, to_updates):
            values = [stage(g, value) for g, value in zip(groups, values)]
        return carry

    lax.fori_loop(0, leds // (group * beside), step, 0)

    def place(led, carry):
        chunk, shift, row = place_of(led)
        for side in range(2):
            moved = pltpu.roll(updates[led, side], shift, 1)
            first[side, chunk, pl.ds(row, window), :] += jnp.where(lane >= shift, moved, 0.0)
            first[side, chunk + 1, pl.ds(row, window), :] += jnp.where(lane >= shift, 0.0, moved)
        return carry

    lax.fori_loop(0, leds, place, 0, unroll=4)
    tile_pass(from_first, second, table, 1)
    transpose_all(second, first)
    tile_pass(from_first, second, table, 1)
    whole = (length - OVL) // LANES
    count, _, rows, _ = late.shape

    def emit(target, part, row, gain):
        here = pl.ds(row, rows)
        for side in range(2):
            for chunk in range(whole):
                target[part, side * whole + chunk] = scaled(second[side, chunk, here, :], gain)
        near = second[0, whole, here, :]
        far = pltpu.roll(second[1, whole, here, :], OVL, 1)
        low = lax.broadcasted_iota(jnp.int32, near.shape, 1) < OVL
        target[part, 2 * whole] = scaled(jnp.where(low, near, far), gain)

    for part in range(count):
        segment, offset = divmod(part * rows, OVL)
        emit(late, part, segment * LANES + OVL + offset, None)
        ramp = None
        if segment == 0:
            ramp = ramp_of(offset + lax.broadcasted_iota(jnp.int32, (rows, LANES), 0))
            emit(below, part, whole * LANES + offset, 1.0 - ramp)
        emit(early, part, segment * LANES + offset, ramp)


def scaled(value, gain):
    return value if gain is None else value * gain


def ramp_of(index):
    return (index.astype(F32) + 0.5) / OVL


def spread_kernel(place, early, above, *outs):
    *outs, token = outs
    token[...] = jnp.zeros(token.shape, F32)
    blended = above.shape[0]
    for step, out in enumerate(outs):
        part = jnp.bitwise_xor(place[0], step)
        out[...] = early[part]

        @pl.when(part < blended)
        def _():
            out[...] += above[jnp.minimum(part, blended - 1)]


UNROLL = 8
GROUP = 4
BESIDE = 4


def gather_kernel(place, finished, *refs):
    *blocks, table, out, values, held = refs
    rows = finished.shape[2]
    for step, block in enumerate(blocks):
        values[jnp.bitwise_xor(place[0], step)] = block[...]
    out[:, :, pl.ds(0, rows), :] = finished[...]
    col_kernel(values, table, out.at[:, :, pl.ds(rows, rows), :], held)


def after_kernel(after, *refs):
    del after
    col_kernel(*refs)


def col_kernel(values, table, out, held):
    tiles, pieces, rows, _ = values.shape
    whole = (pieces - 1) // 2
    width = out.shape[3] // 2
    per = LANES // width

    def enter(strip, carry):
        here = pl.ds(pl.multiple_of(strip * 8, 8), 8)
        lane = lax.broadcasted_iota(jnp.int32, (8, LANES), 1)
        ramp = jnp.where(lane < OVL, ramp_of(lane), 1.0)
        rest = 1.0 - ramp
        segments = []
        for tile in range(tiles):
            halo = values[(tile - 1) % tiles, 2 * whole, here, :]
            for chunk in range(whole):
                real = values[tile, chunk, here, :]
                imag = values[tile, whole + chunk, here, :]
                if chunk == 0:
                    real = ramp * real + rest * halo
                    imag = ramp * imag + rest * pltpu.roll(halo, OVL, 1)
                segments.append((real, imag))
        for index, (real, imag) in enumerate(short_fft(segments, -1)):
            held[index, 0, here, :] = real
            held[index, 1, here, :] = imag
        return carry

    lax.fori_loop(0, rows // 8, enter, 0)

    def multiply(index, carry):
        value = held[index].reshape(2 * rows, LANES)
        high = value.astype(BF16)
        both = jnp.concatenate([value, value - high.astype(F32)], axis=0).astype(BF16)
        main = jnp.dot(both, table[0, index], preferred_element_type=F32)
        rest = jnp.dot(high, table[1, index], preferred_element_type=F32)
        full = main[: 2 * rows] + (main[2 * rows :] + rest)
        held[index, 0] = full[:rows, :LANES] - full[rows:, LANES:]
        held[index, 1] = full[:rows, LANES:] + full[rows:, :LANES]
        return carry

    lax.fori_loop(0, tiles * whole, multiply, 0, unroll=UNROLL)

    def leave(strip, carry):
        here = pl.ds(pl.multiple_of(strip * 8, 8), 8)
        segments = [
            (held[index, 0, here, :], held[index, 1, here, :]) for index in range(tiles * whole)
        ]
        for index, (real, imag) in enumerate(short_fft(segments, 1)):
            tile, chunk = index // whole, index % whole
            for piece in range(per):
                cut = slice(piece * width, (piece + 1) * width)
                out[chunk * per + piece, tile, here, pl.ds(0, width)] = real[:, cut]
                out[chunk * per + piece, tile, here, pl.ds(width, width)] = imag[:, cut]
        return carry

    lax.fori_loop(0, rows // 8, leave, 0)


def row_kernel(half, place, values, table, *refs):
    *outs, held = refs
    tiles, _, both = values.shape
    width = both // 2
    stride = outs[0].shape[0]
    part = table.shape[3] // 2
    whole = stride // part

    def enter_from(offset, first):
        def enter(strip, carry):
            segments = []
            for tile in range(tiles):
                for chunk in range(whole):
                    row = chunk * OVL + strip * 8
                    row = row // half * (2 * half) + lax.rem(row, half) + offset
                    value = values[tile, pl.ds(pl.multiple_of(row, 8), 8), :]
                    segments.append((value[:, :width], value[:, width:]))
            here = pl.ds(pl.multiple_of(first + strip * 8, 8), 8)
            for index, (real, imag) in enumerate(short_fft(segments, -1)):
                held[index, here, :] = real
                held[index, pl.ds(pl.multiple_of(part + first + strip * 8, 8), 8), :] = imag
            return carry

        lax.fori_loop(0, OVL // 8, enter, 0)

    enter_from(half, 0)
    enter_from(0, OVL)

    def multiply(index, carry):
        high, low = split(held[index])
        main = jnp.dot(
            table[0, index], jnp.concatenate([high, low], axis=1), preferred_element_type=F32
        )
        rest = jnp.dot(table[1, index], high, preferred_element_type=F32)
        held[index] = main[:, :width] + (main[:, width:] + rest)
        return carry

    lax.fori_loop(0, tiles * whole, multiply, 0, unroll=UNROLL)

    def leave_as(me):
        def leave(strip, carry):
            here = pl.ds(pl.multiple_of(strip * 8, 8), 8)
            segments = []
            for index in range(tiles * whole):
                below = pl.ds(pl.multiple_of(part + strip * 8, 8), 8)
                segments.append((held[index, here, :], held[index, below, :]))
            for index, (real, imag) in enumerate(short_fft(segments, 1)):
                tile, chunk = index // whole, index % whole
                here = pl.ds(pl.multiple_of(chunk * part + strip * 8, 8), 8)
                outs[tile ^ me][here, pl.ds(0, width)] = real
                outs[tile ^ me][here, pl.ds(width, width)] = imag
            return carry

        @pl.when(place[1] == me)
        def _():
            lax.fori_loop(0, part // 8, leave, 0)

    for me in range(tiles):
        leave_as(me)


def join_kernel(place, *refs):
    *blocks, out, ordered, done = refs
    width = blocks[0].shape[1] // 2
    if width % LANES:
        for step, block in enumerate(blocks):
            part = jnp.bitwise_xor(place[1], step)
            ordered[part] = block[...]
        for part in range(len(blocks)):
            for side in range(2):
                lanes = pl.ds(part * width, width)
                out[side, :, lanes] = ordered[part, :, pl.ds(side * width, width)]
        return
    copies = []
    for step, block in enumerate(blocks):
        part = jnp.bitwise_xor(place[1], step)
        lanes = pl.ds(pl.multiple_of(part * width, LANES), width)
        for side in range(2):
            copies.append(
                pltpu.make_async_copy(
                    block.at[:, pl.ds(side * width, width)],
                    out.at[side, :, lanes],
                    done.at[len(copies)],
                )
            )
            copies[-1].start()
    for copy in copies:
        copy.wait()


VMEM = pl.BlockSpec(memory_space=pltpu.VMEM)
SMEM = pl.BlockSpec(memory_space=pltpu.SMEM)
HBM = pl.BlockSpec(memory_space=pltpu.HBM)


def call(kernel, shapes, scratch, limit, micros, *operands, scalars=0, outside=()):
    return pl.pallas_call(
        kernel,
        out_shape=[jax.ShapeDtypeStruct(shape, F32) for shape in shapes],
        in_specs=[
            SMEM if place < scalars else HBM if place - len(operands) in outside else VMEM
            for place in range(len(operands))
        ],
        out_specs=[VMEM] * len(shapes),
        scratch_shapes=scratch,
        cost_estimate=pl.CostEstimate(
            flops=int(micros * 5e8), bytes_accessed=int(micros * 2e6), transcendentals=0
        ),
        compiler_params=pltpu.CompilerParams(vmem_limit_bytes=limit << 20),
    )(*operands)


def local(row_count, col_count, tiles, pupils, intensity, offsets):
    length = tiles.shape[1]
    window = pupils.shape[1]
    leds = intensity.shape[0]
    stride = length - OVL
    whole = stride // LANES
    chunks = whole + 1
    rows = stride // (2 * col_count)
    width = stride // row_count
    fresnel = stride * row_count // 2
    block = (2 * whole + 1, rows, LANES)
    operands = (
        tiles,
        tile_tables(length),
        pupils,
        intensity,
        along_right(right_block(dft_matrix(window))),
        along_left(left_block(dft_matrix(window))),
    )
    buffer = pltpu.VMEM((2, chunks, length, LANES), F32)
    late, early, below = call(
        refine_kernel,
        [(col_count, *block), (col_count, *block), (OVL // rows, *block)],
        [pltpu.VMEM(operand.shape, operand.dtype) for operand in operands]
        + [
            buffer,
            buffer,
            pltpu.VMEM((leds, 2, window, window), F32),
            pltpu.SemaphoreType.DMA((chunks,)),
            pltpu.SemaphoreType.DMA((len(operands) - 1,)),
        ],
        56,
        22,
        offsets[0, 0],
        *operands,
        scalars=1,
        outside=range(-len(operands), 0),
    )
    above = lax.ppermute(below, "row", [(r, (r + 1) % row_count) for r in range(row_count)])
    late = lax.all_to_all(late, "col", split_axis=0, concat_axis=0, tiled=True)
    place = jnp.stack([lax.axis_index("col"), lax.axis_index("row")]).astype(jnp.int32)
    *early, token = call(
        spread_kernel, [block] * col_count + [(8, LANES)], [], 16, 40, place, early, above, scalars=1
    )
    early = [early[0]] + [
        lax.ppermute(early[step], "col", [(c, c ^ step) for c in range(col_count)])
        for step in range(1, col_count)
    ]
    col_classes = col_count * whole
    table = spread_tables(stride * col_count, fresnel, col_classes, lambda m: right_half(m.T))
    scratch = [pltpu.VMEM((col_classes, 2, rows, LANES), F32)]
    (field,) = call(
        after_kernel,
        [(row_count, col_count, rows, 2 * width)],
        scratch,
        32,
        4,
        token,
        late,
        table,
        outside=(-3,),
    )
    (field,) = call(
        gather_kernel,
        [(row_count, col_count, 2 * rows, 2 * width)],
        [pltpu.VMEM((col_count, *block), F32)] + scratch,
        32,
        4,
        place,
        field,
        *early,
        table,
        scalars=1,
    )
    field = field.reshape(row_count * col_count, 2 * rows, 2 * width)
    field = lax.all_to_all(field, ("row", "col"), split_axis=0, concat_axis=0, tiled=True)
    row_classes = row_count * whole
    table = spread_tables(stride * row_count, fresnel, row_classes, left_block)
    shape = (stride, 2 * width)
    blocks = call(
        functools.partial(row_kernel, rows),
        [shape] * row_count,
        [
            pltpu.VMEM((row_classes, 2 * LANES, width), F32),
        ],
        32,
        5,
        place,
        field.reshape(row_count, col_count * 2 * rows, 2 * width),
        table,
        scalars=1,
    )
    blocks = [blocks[0]] + [
        lax.ppermute(blocks[step], "row", [(r, r ^ step) for r in range(row_count)])
        for step in range(1, row_count)
    ]
    return pl.pallas_call(
        join_kernel,
        out_shape=jax.ShapeDtypeStruct((2, stride, stride), F32),
        in_specs=[SMEM] + [VMEM] * row_count,
        out_specs=VMEM if width % LANES else HBM,
        scratch_shapes=[
            pltpu.VMEM((row_count, *shape) if width % LANES else (8, LANES), F32),
            pltpu.SemaphoreType.DMA((2 * row_count,)),
        ],
        compiler_params=pltpu.CompilerParams(vmem_limit_bytes=16 << 20),
    )(place, *blocks)


def solution(mesh):
    placed = (
        P(None, "row", "col"),
        P(None, "row", "col"),
        P(None, "row", "col"),
        P("row", "col", None, None),
    )
    return jax.shard_map(
        functools.partial(local, mesh.shape["row"], mesh.shape["col"]),
        mesh=mesh,
        in_specs=placed,
        out_specs=P(None, "row", "col"),
        check_vma=False,
    )
```

```python
import functools
import math

import jax
import jax.numpy as jnp
import ml_dtypes
import numpy as np
from jax import lax
from jax.experimental import pallas as pl
from jax.experimental.pallas import tpu as pltpu
from jax.sharding import PartitionSpec as P

OVL = 64
STEP_SIZE = 0.05
LANES = 128
RADIX = 8
BF16 = jnp.bfloat16
F32 = jnp.float32


def halves(table):
    table = np.asarray(table, np.float64)
    high = table.astype(np.float32).astype(ml_dtypes.bfloat16)
    low = (table - high.astype(np.float64)).astype(np.float32).astype(ml_dtypes.bfloat16)
    return high, low


def left_half(matrix):
    return np.concatenate([matrix.real, matrix.imag], axis=0)


def right_half(matrix):
    return np.concatenate([matrix.real, matrix.imag], axis=1)


def left_block(matrix):
    return np.block([[matrix.real, -matrix.imag], [matrix.imag, matrix.real]])


def right_block(matrix):
    return np.block([[matrix.real, matrix.imag], [-matrix.imag, matrix.real]])


def along_left(block):
    high, low = halves(block)
    return np.concatenate([high, high, low], axis=-1)


def along_right(block):
    high, low = halves(block)
    return np.concatenate([high, high, low], axis=-2)


def dft_matrix(length):
    index = np.arange(length)
    turns = (index[:, None] * index[None, :]) % length
    return np.exp(-2j * np.pi * turns / length) / math.sqrt(length)


def tile_tables(length):
    part = length // RADIX
    index = np.arange(part)
    tables = []
    for residue in range(RADIX):
        turns = (index[None, :] * (residue + RADIX * index[:, None])) % length
        matrix = np.exp(-2j * np.pi * turns / length) / math.sqrt(length)
        tables.append(along_left(left_half(matrix)))
    return np.stack(tables)


def spread_tables(length, fresnel, count, block_of):
    signed = np.arange(length, dtype=np.float64)
    signed = np.where(signed < length // 2, signed, signed - length)
    square = signed * signed
    turns = square * (fresnel / (length * length))
    turns = turns - np.floor(turns)
    kernel = np.fft.ifft(np.exp(-2.0 * square / (length * length)) * np.exp(-2j * np.pi * turns))
    part = length // count
    shift = np.arange(part)[:, None] - np.arange(part)[None, :]
    places = (np.arange(count)[:, None] * part + np.arange(1 - part, part)[None, :]) % length
    classes = np.fft.fft(kernel[places], axis=0) / count
    pairs = [halves(block_of(line[shift + part - 1])) for line in classes]
    return np.stack([np.stack([pair[0] for pair in pairs]), np.stack([pair[1] for pair in pairs])])


def split(value):
    high = value.astype(BF16)
    low = (value - high.astype(F32)).astype(BF16)
    return high, low


def turned(value, eighth_turns, sign):
    real, imag = value
    angle = sign * 2.0 * math.pi * eighth_turns
    if eighth_turns == 0:
        return real, imag
    if eighth_turns == 0.25:
        return (imag, -real) if sign < 0 else (-imag, real)
    cosine, sine = math.cos(angle), math.sin(angle)
    return real * cosine - imag * sine, real * sine + imag * cosine


def short_fft(values, sign):
    count = len(values)
    if count == 1:
        return values
    even = short_fft(values[0::2], sign)
    odd = short_fft(values[1::2], sign)
    low, high = [], []
    for index in range(count // 2):
        real, imag = turned(odd[index], index / count, sign)
        low.append((even[index][0] + real, even[index][1] + imag))
        high.append((even[index][0] - real, even[index][1] - imag))
    return low + high


def tile_pass(load, target, table, sign, after=None):
    part = table.shape[1] // 2
    for chunk in range(target.shape[1]):
        values = [
            tuple(load(side, chunk, pl.ds(part * step, part)) for side in range(2))
            for step in range(RADIX)
        ]
        for residue, value in enumerate(short_fft(values, sign)):
            value = jnp.concatenate(value, axis=1)
            high = value.astype(BF16).astype(F32)
            stacked = jnp.concatenate([high, value - high, high], axis=0).astype(BF16)
            result = jnp.dot(table[residue], stacked, preferred_element_type=F32)
            plain, crossed = result[:part], result[part:]
            real, imag = plain[:, :LANES], plain[:, LANES:]
            if sign < 0:
                real, imag = real - crossed[:, LANES:], imag + crossed[:, :LANES]
            else:
                real, imag = real + crossed[:, LANES:], imag - crossed[:, :LANES]
            rows = pl.ds(residue, part, stride=RADIX)
            target[0, chunk, rows, :] = real
            target[1, chunk, rows, :] = imag
        if after is not None:
            after(chunk)


def transpose_all(source, target):
    chunks, length = source.shape[1], source.shape[2]
    for side in range(2):
        for chunk in range(chunks):
            rows = min(LANES, length - chunk * LANES)
            for other in range(chunks):
                width = min(LANES, length - other * LANES)
                block = source[side, chunk, pl.ds(other * LANES, width), :]
                target[side, other, pl.ds(chunk * LANES, rows), pl.ds(0, width)] = block.T[:rows]


def refine_kernel(starts, *refs):
    sources, results, refs = refs[:6], refs[6:9], refs[9:]
    (late, early, below), sent, refs = refs[:3], refs[3], refs[4:]
    held, (first, second, updates, arrived, done) = refs[:6], refs[6:]
    tiles, table, pupils, intensity, row_table, col_table = held
    length = tiles.shape[1]
    window = pupils.shape[1]
    leds = intensity.shape[0]
    chunks = first.shape[1]
    rest = length - (chunks - 1) * LANES
    tile_copies = []
    for chunk in range(chunks):
        lanes = pl.ds(chunk * LANES, min(LANES, length - chunk * LANES))
        tile_copies.append(
            pltpu.make_async_copy(sources[0].at[:, :, lanes], tiles.at[:, :, lanes], arrived.at[chunk])
        )
    copies = [
        pltpu.make_async_copy(source, target, done.at[place])
        for place, (source, target) in enumerate(zip(sources[1:], held[1:]))
    ]
    tile_copies[0].start()
    copies[0].start()
    for copy in tile_copies[1:] + copies[1:]:
        copy.start()

    def from_tiles(side, chunk, rows):
        if side == 0 and rows.start == 0:
            tile_copies[chunk].wait()
            if chunk == chunks - 1:
                for part in range(2):
                    second[part, chunk, :, pl.ds(0, rest)] = tiles[part, :, pl.ds(chunk * LANES, rest)]
        if chunk == chunks - 1:
            return second[side, chunk, rows, :]
        return tiles[side, rows, pl.ds(chunk * LANES, LANES)]

    def from_first(side, chunk, rows):
        return first[side, chunk, rows, :]

    def from_second(side, chunk, rows):
        return second[side, chunk, rows, :]

    copies[0].wait()
    tile_pass(from_tiles, first, table, -1)
    transpose_all(first, second)
    tile_pass(from_second, first, table, -1)
    for copy in copies[1:]:
        copy.wait()
    lens_real, lens_imag = pupils[0].T, pupils[1].T
    lane = lax.broadcasted_iota(jnp.int32, (window, LANES), 1)
    group, beside = (GROUP, BESIDE) if leds % (GROUP * BESIDE) == 0 else (1, 1)

    def place_of(led):
        start = starts[0, led]
        chunk = start // LANES
        return chunk, start - chunk * LANES, starts[1, led]

    def along_rows(value):
        high, low = split(value)
        return jnp.dot(
            jnp.concatenate([high, low, high], axis=1), row_table[...], preferred_element_type=F32
        )

    def along_cols(value):
        high, low = split(value)
        return jnp.dot(
            col_table[...], jnp.concatenate([high, low, high], axis=0), preferred_element_type=F32
        )

    def crop(led):
        chunk, shift, row = place_of(led)
        crop = []
        for side in range(2):
            here = first[side, chunk, pl.ds(row, window), :]
            beyond = first[side, chunk + 1, pl.ds(row, window), :]
            joined = jnp.where(lane >= shift, here, beyond)
            crop.append(pltpu.roll(joined, lax.rem(LANES - shift, LANES), 1))
        real = lens_real * crop[0] - lens_imag * crop[1]
        imag = -lens_real * crop[1] - lens_imag * crop[0]
        return jnp.concatenate([real, imag], axis=1)

    def to_waves(leds):
        return along_rows(jnp.concatenate([crop(led) for led in leds], axis=0))

    def to_wave_cols(leds, wave):
        blocks = [wave[m * window : (m + 1) * window] for m in range(len(leds))]
        blocks = [jnp.concatenate([b[:, :window], b[:, window:]], axis=0) for b in blocks]
        return along_cols(jnp.concatenate(blocks, axis=1))

    def to_grad_cols(leds, wave):
        real, imag = wave[:window], wave[window:]
        measured = jnp.concatenate([intensity[led].T for led in leds], axis=1)
        excess = real * real + imag * imag - measured
        return along_cols(jnp.concatenate([real * excess, -imag * excess], axis=0))

    def to_grads(leds, grad):
        blocks = [grad[:, m * window : (m + 1) * window] for m in range(len(leds))]
        blocks = [jnp.concatenate([b[:window], b[window:]], axis=1) for b in blocks]
        return along_rows(jnp.concatenate(blocks, axis=0))

    def to_updates(leds, grad):
        for m, led in enumerate(leds):
            real = grad[m * window : (m + 1) * window, :window]
            imag = grad[m * window : (m + 1) * window, window:]
            updates[led, 0] = -STEP_SIZE * (lens_real * real + lens_imag * imag)
            updates[led, 1] = -STEP_SIZE * (lens_real * imag - lens_imag * real)

    def step(index, carry):
        groups = [
            [(index * beside + g) * group + m for m in range(group)] for g in range(beside)
        ]
        values = [to_waves(g) for g in groups]
        for stage in (to_wave_cols, to_grad_cols, to_grads, to_updates):
            values = [stage(g, value) for g, value in zip(groups, values)]
        return carry

    lax.fori_loop(0, leds // (group * beside), step, 0)

    def place(led, carry):
        chunk, shift, row = place_of(led)
        for side in range(2):
            moved = pltpu.roll(updates[led, side], shift, 1)
            first[side, chunk, pl.ds(row, window), :] += jnp.where(lane >= shift, moved, 0.0)
            first[side, chunk + 1, pl.ds(row, window), :] += jnp.where(lane >= shift, 0.0, moved)
        return carry

    lax.fori_loop(0, leds, place, 0, unroll=8)
    tile_pass(from_first, second, table, 1)
    transpose_all(second, first)
    whole = (length - OVL) // LANES
    count, _, rows, _ = late.shape
    sends = []

    def emit(chunk):
        def put(target, piece, part, row, gain):
            here = pl.ds(row, rows)
            if chunk < whole:
                value = second[piece // whole, chunk, here, :]
            else:
                far = pltpu.roll(second[1, whole, here, :], OVL, 1)
                low = lax.broadcasted_iota(jnp.int32, far.shape, 1) < OVL
                value = jnp.where(low, second[0, whole, here, :], far)
            target[part, piece] = scaled(value, gain)

        for piece in (chunk, whole + chunk) if chunk < whole else (2 * whole,):
            for part in range(count):
                segment, offset = divmod(part * rows, OVL)
                put(late, piece, part, segment * LANES + OVL + offset, None)
                ramp = None
                if segment == 0:
                    ramp = ramp_of(offset + lax.broadcasted_iota(jnp.int32, (rows, LANES), 0))
                    put(below, piece, part, whole * LANES + offset, 1.0 - ramp)
                put(early, piece, part, segment * LANES + offset, ramp)
            for source, target in zip((late, early, below), results):
                sends.append(
                    pltpu.make_async_copy(
                        source.at[:, piece], target.at[:, piece], sent.at[len(sends)]
                    )
                )
                sends[-1].start()

    tile_pass(from_first, second, table, 1, emit)
    for copy in sends:
        copy.wait()


def scaled(value, gain):
    return value if gain is None else value * gain


def ramp_of(index):
    return (index.astype(F32) + 0.5) / OVL


def spread_kernel(place, early, above, *outs):
    *outs, token = outs
    token[...] = jnp.zeros(token.shape, F32)
    blended = above.shape[0]
    for step, out in enumerate(outs):
        part = jnp.bitwise_xor(place[0], step)
        out[...] = early[part]

        @pl.when(part < blended)
        def _():
            out[...] += above[jnp.minimum(part, blended - 1)]


UNROLL = 16
GROUP = 4
BESIDE = 4


def gather_kernel(place, finished, *refs):
    *blocks, table, out, values, held, done = refs
    rows = finished.shape[2]
    copy = pltpu.make_async_copy(finished, out.at[:, :, pl.ds(0, rows), :], done)
    copy.start()
    for step, block in enumerate(blocks):
        values[jnp.bitwise_xor(place[0], step)] = block[...]
    col_kernel(values, table, out.at[:, :, pl.ds(rows, rows), :], held)
    copy.wait()


def after_kernel(after, *refs):
    del after
    col_kernel(*refs)


def col_kernel(values, table, out, held):
    tiles, pieces, rows, _ = values.shape
    whole = (pieces - 1) // 2
    width = out.shape[3] // 2
    per = LANES // width

    def enter(strip, carry):
        here = pl.ds(pl.multiple_of(strip * 8, 8), 8)
        lane = lax.broadcasted_iota(jnp.int32, (8, LANES), 1)
        ramp = jnp.where(lane < OVL, ramp_of(lane), 1.0)
        rest = 1.0 - ramp
        segments = []
        for tile in range(tiles):
            halo = values[(tile - 1) % tiles, 2 * whole, here, :]
            for chunk in range(whole):
                real = values[tile, chunk, here, :]
                imag = values[tile, whole + chunk, here, :]
                if chunk == 0:
                    real = ramp * real + rest * halo
                    imag = ramp * imag + rest * pltpu.roll(halo, OVL, 1)
                segments.append((real, imag))
        for index, (real, imag) in enumerate(short_fft(segments, -1)):
            held[index, 0, here, :] = real
            held[index, 1, here, :] = imag
        return carry

    lax.fori_loop(0, rows // 8, enter, 0)

    def multiply(index, carry):
        value = held[index].reshape(2 * rows, LANES)
        high = value.astype(BF16)
        both = jnp.concatenate([value, value - high.astype(F32)], axis=0).astype(BF16)
        main = jnp.dot(both, table[0, index], preferred_element_type=F32)
        rest = jnp.dot(high, table[1, index], preferred_element_type=F32)
        full = main[: 2 * rows] + (main[2 * rows :] + rest)
        held[index, 0] = full[:rows, :LANES] - full[rows:, LANES:]
        held[index, 1] = full[:rows, LANES:] + full[rows:, :LANES]
        return carry

    lax.fori_loop(0, tiles * whole, multiply, 0, unroll=UNROLL)

    def leave(strip, carry):
        here = pl.ds(pl.multiple_of(strip * 8, 8), 8)
        segments = [
            (held[index, 0, here, :], held[index, 1, here, :]) for index in range(tiles * whole)
        ]
        for index, (real, imag) in enumerate(short_fft(segments, 1)):
            tile, chunk = index // whole, index % whole
            for piece in range(per):
                cut = slice(piece * width, (piece + 1) * width)
                out[chunk * per + piece, tile, here, pl.ds(0, width)] = real[:, cut]
                out[chunk * per + piece, tile, here, pl.ds(width, width)] = imag[:, cut]
        return carry

    lax.fori_loop(0, rows // 8, leave, 0)


def row_kernel(half, place, values, table, *refs):
    *outs, held = refs
    tiles, _, both = values.shape
    width = both // 2
    stride = outs[0].shape[0]
    part = table.shape[3] // 2
    whole = stride // part

    def enter_from(offset, first):
        def enter(strip, carry):
            segments = []
            for tile in range(tiles):
                for chunk in range(whole):
                    row = chunk * OVL + strip * 8
                    row = row // half * (2 * half) + lax.rem(row, half) + offset
                    value = values[tile, pl.ds(pl.multiple_of(row, 8), 8), :]
                    segments.append((value[:, :width], value[:, width:]))
            here = pl.ds(pl.multiple_of(first + strip * 8, 8), 8)
            for index, (real, imag) in enumerate(short_fft(segments, -1)):
                held[index, here, :] = real
                held[index, pl.ds(pl.multiple_of(part + first + strip * 8, 8), 8), :] = imag
            return carry

        lax.fori_loop(0, OVL // 8, enter, 0)

    enter_from(half, 0)
    enter_from(0, OVL)

    def multiply(index, carry):
        high, low = split(held[index])
        main = jnp.dot(
            table[0, index], jnp.concatenate([high, low], axis=1), preferred_element_type=F32
        )
        rest = jnp.dot(table[1, index], high, preferred_element_type=F32)
        held[index] = main[:, :width] + (main[:, width:] + rest)
        return carry

    lax.fori_loop(0, tiles * whole, multiply, 0, unroll=UNROLL)

    def leave_as(me):
        def leave(strip, carry):
            here = pl.ds(pl.multiple_of(strip * 8, 8), 8)
            segments = []
            for index in range(tiles * whole):
                below = pl.ds(pl.multiple_of(part + strip * 8, 8), 8)
                segments.append((held[index, here, :], held[index, below, :]))
            for index, (real, imag) in enumerate(short_fft(segments, 1)):
                tile, chunk = index // whole, index % whole
                here = pl.ds(pl.multiple_of(chunk * part + strip * 8, 8), 8)
                outs[tile ^ me][here, pl.ds(0, width)] = real
                outs[tile ^ me][here, pl.ds(width, width)] = imag
            return carry

        @pl.when(place[1] == me)
        def _():
            lax.fori_loop(0, part // 8, leave, 0)

    for me in range(tiles):
        leave_as(me)


def join_kernel(steps, place, *refs):
    blocks, out, done = refs[: len(steps)], refs[-2], refs[-1]
    width = blocks[0].shape[1] // 2
    copies = []
    for step, block in zip(steps, blocks):
        part = jnp.bitwise_xor(place[1], step)
        lanes = pl.ds(pl.multiple_of(part * width, LANES), width)
        for side in range(2):
            copies.append(
                pltpu.make_async_copy(
                    block.at[:, pl.ds(side * width, width)],
                    out.at[side, :, lanes],
                    done.at[len(copies)],
                )
            )
            copies[-1].start()
    for copy in copies:
        copy.wait()


def narrow_join_kernel(place, *refs):
    *blocks, out, ordered = refs
    width = blocks[0].shape[1] // 2
    for step, block in enumerate(blocks):
        ordered[jnp.bitwise_xor(place[1], step)] = block[...]
    for part in range(len(blocks)):
        for side in range(2):
            lanes = pl.ds(part * width, width)
            out[side, :, lanes] = ordered[part, :, pl.ds(side * width, width)]


VMEM = pl.BlockSpec(memory_space=pltpu.VMEM)
SMEM = pl.BlockSpec(memory_space=pltpu.SMEM)
HBM = pl.BlockSpec(memory_space=pltpu.HBM)


def call(kernel, shapes, scratch, limit, micros, *operands, scalars=0, outside=(), to=None):
    return pl.pallas_call(
        kernel,
        out_shape=[jax.ShapeDtypeStruct(shape, F32) for shape in shapes],
        in_specs=[
            SMEM if place < scalars else HBM if place - len(operands) in outside else VMEM
            for place in range(len(operands))
        ],
        out_specs=[to or VMEM] * len(shapes),
        scratch_shapes=scratch,
        cost_estimate=pl.CostEstimate(
            flops=int(micros * 5e8), bytes_accessed=int(micros * 2e6), transcendentals=0
        ),
        compiler_params=pltpu.CompilerParams(vmem_limit_bytes=limit << 20),
    )(*operands)


def local(row_count, col_count, tiles, pupils, intensity, offsets):
    length = tiles.shape[1]
    window = pupils.shape[1]
    leds = intensity.shape[0]
    stride = length - OVL
    whole = stride // LANES
    chunks = whole + 1
    rows = stride // (2 * col_count)
    width = stride // row_count
    fresnel = stride * row_count // 2
    block = (2 * whole + 1, rows, LANES)
    operands = (
        tiles,
        tile_tables(length),
        pupils,
        intensity,
        along_right(right_block(dft_matrix(window))),
        along_left(left_block(dft_matrix(window))),
    )
    buffer = pltpu.VMEM((2, chunks, length, LANES), F32)
    results = [(col_count, *block), (col_count, *block), (OVL // rows, *block)]
    late, early, below = call(
        refine_kernel,
        results,
        [pltpu.VMEM(shape, F32) for shape in results]
        + [pltpu.SemaphoreType.DMA((len(results) * block[0],))]
        + [pltpu.VMEM(operand.shape, operand.dtype) for operand in operands]
        + [
            buffer,
            buffer,
            pltpu.VMEM((leds, 2, window, window), F32),
            pltpu.SemaphoreType.DMA((chunks,)),
            pltpu.SemaphoreType.DMA((len(operands) - 1,)),
        ],
        56,
        22,
        offsets[0, 0],
        *operands,
        scalars=1,
        outside=range(-len(operands), 0),
        to=HBM,
    )
    above = lax.ppermute(below, "row", [(r, (r + 1) % row_count) for r in range(row_count)])
    late = lax.all_to_all(late, "col", split_axis=0, concat_axis=0, tiled=True)
    place = jnp.stack([lax.axis_index("col"), lax.axis_index("row")]).astype(jnp.int32)
    *early, token = call(
        spread_kernel, [block] * col_count + [(8, LANES)], [], 16, 40, place, early, above, scalars=1
    )
    early = [early[0]] + [
        lax.ppermute(early[step], "col", [(c, c ^ step) for c in range(col_count)])
        for step in range(1, col_count)
    ]
    col_classes = col_count * whole
    table = spread_tables(stride * col_count, fresnel, col_classes, lambda m: right_half(m.T))
    scratch = [pltpu.VMEM((col_classes, 2, rows, LANES), F32)]
    (field,) = call(
        after_kernel,
        [(row_count, col_count, rows, 2 * width)],
        scratch,
        32,
        4,
        token,
        late,
        table,
        outside=(-3,),
    )
    (field,) = call(
        gather_kernel,
        [(row_count, col_count, 2 * rows, 2 * width)],
        [pltpu.VMEM((col_count, *block), F32)] + scratch + [pltpu.SemaphoreType.DMA],
        32,
        4,
        place,
        field,
        *early,
        table,
        scalars=1,
    )
    field = field.reshape(row_count * col_count, 2 * rows, 2 * width)
    field = lax.all_to_all(field, ("row", "col"), split_axis=0, concat_axis=0, tiled=True)
    row_classes = row_count * whole
    table = spread_tables(stride * row_count, fresnel, row_classes, left_block)
    shape = (stride, 2 * width)
    blocks = call(
        functools.partial(row_kernel, rows),
        [shape] * row_count,
        [
            pltpu.VMEM((row_classes, 2 * LANES, width), F32),
        ],
        32,
        5,
        place,
        field.reshape(row_count, col_count * 2 * rows, 2 * width),
        table,
        scalars=1,
    )
    blocks = [blocks[0]] + [
        lax.ppermute(blocks[step], "row", [(r, r ^ step) for r in range(row_count)])
        for step in range(1, row_count)
    ]
    whole_shape = (2, stride, stride)
    if width % LANES:
        scratch = [pltpu.VMEM((row_count, *shape), F32)]
        (field,) = call(
            narrow_join_kernel, [whole_shape], scratch, 32, 2, place, *blocks, scalars=1
        )
        return field

    def join(steps, field):
        prior = [] if field is None else [field]
        return pl.pallas_call(
            functools.partial(join_kernel, steps),
            out_shape=jax.ShapeDtypeStruct(whole_shape, F32),
            in_specs=[SMEM] + [VMEM] * len(steps) + [HBM] * len(prior),
            out_specs=HBM,
            scratch_shapes=[pltpu.SemaphoreType.DMA((2 * len(steps),))],
            input_output_aliases={1 + len(steps): 0} if prior else {},
            compiler_params=pltpu.CompilerParams(vmem_limit_bytes=16 << 20),
        )(place, *[blocks[step] for step in steps], *prior)

    return join([row_count - 1], join(range(row_count - 1), None))


def solution(mesh):
    placed = (
        P(None, "row", "col"),
        P(None, "row", "col"),
        P(None, "row", "col"),
        P("row", "col", None, None),
    )
    return jax.shard_map(
        functools.partial(local, mesh.shape["row"], mesh.shape["col"]),
        mesh=mesh,
        in_specs=placed,
        out_specs=P(None, "row", "col"),
        check_vma=False,
    )
```

```python
import functools
import math

import jax
import jax.numpy as jnp
import ml_dtypes
import numpy as np
from jax import lax
from jax.experimental import pallas as pl
from jax.experimental.pallas import tpu as pltpu
from jax.sharding import PartitionSpec as P

OVL = 64
STEP_SIZE = 0.05
LANES = 128
RADIX = 8
BF16 = jnp.bfloat16
F32 = jnp.float32


def halves(table):
    table = np.asarray(table, np.float64)
    high = table.astype(np.float32).astype(ml_dtypes.bfloat16)
    low = (table - high.astype(np.float64)).astype(np.float32).astype(ml_dtypes.bfloat16)
    return high, low


def left_half(matrix):
    return np.concatenate([matrix.real, matrix.imag], axis=0)


def right_half(matrix):
    return np.concatenate([matrix.real, matrix.imag], axis=1)


def left_block(matrix):
    return np.block([[matrix.real, -matrix.imag], [matrix.imag, matrix.real]])


def right_block(matrix):
    return np.block([[matrix.real, matrix.imag], [-matrix.imag, matrix.real]])


def along_left(block):
    high, low = halves(block)
    return np.concatenate([high, high, low], axis=-1)


def along_right(block):
    high, low = halves(block)
    return np.concatenate([high, high, low], axis=-2)


def dft_matrix(length):
    index = np.arange(length)
    turns = (index[:, None] * index[None, :]) % length
    return np.exp(-2j * np.pi * turns / length) / math.sqrt(length)


def tile_tables(length):
    part = length // RADIX
    index = np.arange(part)
    tables = []
    for residue in range(RADIX):
        turns = (index[None, :] * (residue + RADIX * index[:, None])) % length
        matrix = np.exp(-2j * np.pi * turns / length) / math.sqrt(length)
        tables.append(along_left(left_half(matrix)))
    return np.stack(tables)


def spread_tables(length, fresnel, count, block_of):
    signed = np.arange(length, dtype=np.float64)
    signed = np.where(signed < length // 2, signed, signed - length)
    square = signed * signed
    turns = square * (fresnel / (length * length))
    turns = turns - np.floor(turns)
    kernel = np.fft.ifft(np.exp(-2.0 * square / (length * length)) * np.exp(-2j * np.pi * turns))
    part = length // count
    shift = np.arange(part)[:, None] - np.arange(part)[None, :]
    places = (np.arange(count)[:, None] * part + np.arange(1 - part, part)[None, :]) % length
    classes = np.fft.fft(kernel[places], axis=0) / count
    pairs = [halves(block_of(line[shift + part - 1])) for line in classes]
    return np.stack([np.stack([pair[0] for pair in pairs]), np.stack([pair[1] for pair in pairs])])


def split(value):
    high = value.astype(BF16)
    low = (value - high.astype(F32)).astype(BF16)
    return high, low


def turned(value, eighth_turns, sign):
    real, imag = value
    angle = sign * 2.0 * math.pi * eighth_turns
    if eighth_turns == 0:
        return real, imag
    if eighth_turns == 0.25:
        return (imag, -real) if sign < 0 else (-imag, real)
    cosine, sine = math.cos(angle), math.sin(angle)
    return real * cosine - imag * sine, real * sine + imag * cosine


def short_fft(values, sign):
    count = len(values)
    if count == 1:
        return values
    even = short_fft(values[0::2], sign)
    odd = short_fft(values[1::2], sign)
    low, high = [], []
    for index in range(count // 2):
        real, imag = turned(odd[index], index / count, sign)
        low.append((even[index][0] + real, even[index][1] + imag))
        high.append((even[index][0] - real, even[index][1] - imag))
    return low + high


def tile_pass(load, target, table, sign, after=None):
    part = table.shape[1] // 2
    for chunk in range(target.shape[1]):
        values = [
            tuple(load(side, chunk, pl.ds(part * step, part)) for side in range(2))
            for step in range(RADIX)
        ]
        for residue, value in enumerate(short_fft(values, sign)):
            value = jnp.concatenate(value, axis=1)
            high = value.astype(BF16).astype(F32)
            stacked = jnp.concatenate([high, value - high, high], axis=0).astype(BF16)
            result = jnp.dot(table[residue], stacked, preferred_element_type=F32)
            plain, crossed = result[:part], result[part:]
            real, imag = plain[:, :LANES], plain[:, LANES:]
            if sign < 0:
                real, imag = real - crossed[:, LANES:], imag + crossed[:, :LANES]
            else:
                real, imag = real + crossed[:, LANES:], imag - crossed[:, :LANES]
            rows = pl.ds(residue, part, stride=RADIX)
            target[0, chunk, rows, :] = real
            target[1, chunk, rows, :] = imag
        if after is not None:
            after(chunk)


def transpose_all(source, target):
    chunks, length = source.shape[1], source.shape[2]
    for side in range(2):
        for chunk in range(chunks):
            rows = min(LANES, length - chunk * LANES)
            for other in range(chunks):
                width = min(LANES, length - other * LANES)
                block = source[side, chunk, pl.ds(other * LANES, width), :]
                target[side, other, pl.ds(chunk * LANES, rows), pl.ds(0, width)] = block.T[:rows]


def refine_kernel(starts, *refs):
    sources, results, refs = refs[:6], refs[6:9], refs[9:]
    (late, early, below), sent, refs = refs[:3], refs[3], refs[4:]
    held, (first, second, updates, arrived, done) = refs[:6], refs[6:]
    tiles, table, pupils, intensity, row_table, col_table = held
    length = tiles.shape[1]
    window = pupils.shape[1]
    leds = intensity.shape[0]
    chunks = first.shape[1]
    rest = length - (chunks - 1) * LANES
    tile_copies = []
    for chunk in range(chunks):
        lanes = pl.ds(chunk * LANES, min(LANES, length - chunk * LANES))
        tile_copies.append(
            pltpu.make_async_copy(sources[0].at[:, :, lanes], tiles.at[:, :, lanes], arrived.at[chunk])
        )
    copies = [
        pltpu.make_async_copy(source, target, done.at[place])
        for place, (source, target) in enumerate(zip(sources[1:], held[1:]))
    ]
    tile_copies[0].start()
    copies[0].start()
    for copy in tile_copies[1:] + copies[1:]:
        copy.start()

    def from_tiles(side, chunk, rows):
        if side == 0 and rows.start == 0:
            tile_copies[chunk].wait()
            if chunk == chunks - 1:
                for part in range(2):
                    second[part, chunk, :, pl.ds(0, rest)] = tiles[part, :, pl.ds(chunk * LANES, rest)]
        if chunk == chunks - 1:
            return second[side, chunk, rows, :]
        return tiles[side, rows, pl.ds(chunk * LANES, LANES)]

    def from_first(side, chunk, rows):
        return first[side, chunk, rows, :]

    def from_second(side, chunk, rows):
        return second[side, chunk, rows, :]

    copies[0].wait()
    tile_pass(from_tiles, first, table, -1)
    transpose_all(first, second)
    tile_pass(from_second, first, table, -1)
    for copy in copies[1:]:
        copy.wait()
    lens_real, lens_imag = pupils[0].T, pupils[1].T
    lane = lax.broadcasted_iota(jnp.int32, (window, LANES), 1)
    group, beside = (GROUP, BESIDE) if leds % (GROUP * BESIDE) == 0 else (1, 1)

    def place_of(led):
        start = starts[0, led]
        chunk = start // LANES
        return chunk, start - chunk * LANES, starts[1, led]

    def along_rows(value):
        high, low = split(value)
        return jnp.dot(
            jnp.concatenate([high, low, high], axis=1), row_table[...], preferred_element_type=F32
        )

    def along_cols(value):
        high, low = split(value)
        return jnp.dot(
            col_table[...], jnp.concatenate([high, low, high], axis=0), preferred_element_type=F32
        )

    def crop(led):
        chunk, shift, row = place_of(led)
        crop = []
        for side in range(2):
            here = first[side, chunk, pl.ds(row, window), :]
            beyond = first[side, chunk + 1, pl.ds(row, window), :]
            joined = jnp.where(lane >= shift, here, beyond)
            crop.append(pltpu.roll(joined, lax.rem(LANES - shift, LANES), 1))
        real = lens_real * crop[0] - lens_imag * crop[1]
        imag = -lens_real * crop[1] - lens_imag * crop[0]
        return jnp.concatenate([real, imag], axis=1)

    def to_waves(leds, value):
        return along_rows(jnp.concatenate([crop(led) for led in leds], axis=0))

    def to_wave_cols(leds, wave):
        blocks = [wave[m * window : (m + 1) * window] for m in range(len(leds))]
        blocks = [jnp.concatenate([b[:, :window], b[:, window:]], axis=0) for b in blocks]
        return along_cols(jnp.concatenate(blocks, axis=1))

    def to_grad_cols(leds, wave):
        real, imag = wave[:window], wave[window:]
        measured = jnp.concatenate([intensity[led].T for led in leds], axis=1)
        excess = real * real + imag * imag - measured
        return along_cols(jnp.concatenate([real * excess, -imag * excess], axis=0))

    def to_grads(leds, grad):
        blocks = [grad[:, m * window : (m + 1) * window] for m in range(len(leds))]
        blocks = [jnp.concatenate([b[:window], b[window:]], axis=1) for b in blocks]
        return along_rows(jnp.concatenate(blocks, axis=0))

    def to_updates(leds, grad):
        for m, led in enumerate(leds):
            real = grad[m * window : (m + 1) * window, :window]
            imag = grad[m * window : (m + 1) * window, window:]
            updates[led, 0] = -STEP_SIZE * (lens_real * real + lens_imag * imag)
            updates[led, 1] = -STEP_SIZE * (lens_real * imag - lens_imag * real)

    def place(led, carry):
        chunk, shift, row = place_of(led)
        for side in range(2):
            moved = pltpu.roll(updates[led, side], shift, 1)
            first[side, chunk, pl.ds(row, window), :] += jnp.where(lane >= shift, moved, 0.0)
            first[side, chunk + 1, pl.ds(row, window), :] += jnp.where(lane >= shift, 0.0, moved)
        return carry

    def to_sum(leds, value):
        for led in leds:
            place(led, 0)

    stages = (to_waves, to_wave_cols, to_grad_cols, to_grads, to_updates)
    if group * beside == leds:
        stages = stages + (to_sum,)
        groups = [range(g * group, (g + 1) * group) for g in range(beside)]
        values = [None] * beside
        for stage in stages:
            values = [stage(g, value) for g, value in zip(groups, values)]
    else:

        def step(index, carry):
            groups = [[(index * beside + g) * group + m for m in range(group)] for g in range(beside)]
            values = [None] * beside
            for stage in stages:
                values = [stage(g, value) for g, value in zip(groups, values)]
            return carry

        lax.fori_loop(0, leds // (group * beside), step, 0)
        lax.fori_loop(0, leds, place, 0, unroll=8)
    tile_pass(from_first, second, table, 1)
    transpose_all(second, first)
    whole = (length - OVL) // LANES
    count, _, rows, _ = late.shape
    sends = []

    def emit(chunk):
        def put(target, piece, part, row, gain):
            here = pl.ds(row, rows)
            if chunk < whole:
                value = second[piece // whole, chunk, here, :]
            else:
                far = pltpu.roll(second[1, whole, here, :], OVL, 1)
                low = lax.broadcasted_iota(jnp.int32, far.shape, 1) < OVL
                value = jnp.where(low, second[0, whole, here, :], far)
            target[part, piece] = scaled(value, gain)

        for piece in (chunk, whole + chunk) if chunk < whole else (2 * whole,):
            for part in range(count):
                segment, offset = divmod(part * rows, OVL)
                put(late, piece, part, segment * LANES + OVL + offset, None)
                ramp = None
                if segment == 0:
                    ramp = ramp_of(offset + lax.broadcasted_iota(jnp.int32, (rows, LANES), 0))
                    put(below, piece, part, whole * LANES + offset, 1.0 - ramp)
                put(early, piece, part, segment * LANES + offset, ramp)
            for source, target in zip((late, early, below), results):
                sends.append(
                    pltpu.make_async_copy(
                        source.at[:, piece], target.at[:, piece], sent.at[len(sends)]
                    )
                )
                sends[-1].start()

    tile_pass(from_first, second, table, 1, emit)
    for copy in sends:
        copy.wait()


def scaled(value, gain):
    return value if gain is None else value * gain


def ramp_of(index):
    return (index.astype(F32) + 0.5) / OVL


def order_kernel(place, early, *outs):
    for step, out in enumerate(outs):
        out[...] = early[jnp.bitwise_xor(place[0], step)]


def spread_kernel(place, above, *refs):
    count = len(refs) // 2
    blocks, outs, token = refs[:count], refs[count:-1], refs[-1]
    token[...] = jnp.zeros(token.shape, F32)
    blended = above.shape[0]
    for step, (block, out) in enumerate(zip(blocks, outs)):
        part = jnp.bitwise_xor(place[0], step)
        out[...] = block[...]

        @pl.when(part < blended)
        def _():
            out[...] += above[jnp.minimum(part, blended - 1)]


UNROLL = 16
GROUP = 4
BESIDE = 4


def gather_kernel(place, finished, *refs):
    *blocks, table, out, values, held, done = refs
    rows = finished.shape[2]
    copy = pltpu.make_async_copy(finished, out.at[:, :, pl.ds(0, rows), :], done)
    copy.start()
    for step, block in enumerate(blocks):
        values[jnp.bitwise_xor(place[0], step)] = block[...]
    col_kernel(values, table, out.at[:, :, pl.ds(rows, rows), :], held)
    copy.wait()


def after_kernel(after, *refs):
    del after
    col_kernel(*refs)


def col_kernel(values, table, out, held):
    tiles, pieces, rows, _ = values.shape
    whole = (pieces - 1) // 2
    width = out.shape[3] // 2
    per = LANES // width

    def enter(strip, carry):
        here = pl.ds(pl.multiple_of(strip * 8, 8), 8)
        lane = lax.broadcasted_iota(jnp.int32, (8, LANES), 1)
        ramp = jnp.where(lane < OVL, ramp_of(lane), 1.0)
        rest = 1.0 - ramp
        segments = []
        for tile in range(tiles):
            halo = values[(tile - 1) % tiles, 2 * whole, here, :]
            for chunk in range(whole):
                real = values[tile, chunk, here, :]
                imag = values[tile, whole + chunk, here, :]
                if chunk == 0:
                    real = ramp * real + rest * halo
                    imag = ramp * imag + rest * pltpu.roll(halo, OVL, 1)
                segments.append((real, imag))
        for index, (real, imag) in enumerate(short_fft(segments, -1)):
            held[index, 0, here, :] = real
            held[index, 1, here, :] = imag
        return carry

    lax.fori_loop(0, rows // 8, enter, 0)

    def multiply(index, carry):
        value = held[index].reshape(2 * rows, LANES)
        high = value.astype(BF16)
        both = jnp.concatenate([value, value - high.astype(F32)], axis=0).astype(BF16)
        main = jnp.dot(both, table[0, index], preferred_element_type=F32)
        rest = jnp.dot(high, table[1, index], preferred_element_type=F32)
        full = main[: 2 * rows] + (main[2 * rows :] + rest)
        held[index, 0] = full[:rows, :LANES] - full[rows:, LANES:]
        held[index, 1] = full[:rows, LANES:] + full[rows:, :LANES]
        return carry

    lax.fori_loop(0, tiles * whole, multiply, 0, unroll=UNROLL)

    def leave(strip, carry):
        here = pl.ds(pl.multiple_of(strip * 8, 8), 8)
        segments = [
            (held[index, 0, here, :], held[index, 1, here, :]) for index in range(tiles * whole)
        ]
        for index, (real, imag) in enumerate(short_fft(segments, 1)):
            tile, chunk = index // whole, index % whole
            for piece in range(per):
                cut = slice(piece * width, (piece + 1) * width)
                out[chunk * per + piece, tile, here, pl.ds(0, width)] = real[:, cut]
                out[chunk * per + piece, tile, here, pl.ds(width, width)] = imag[:, cut]
        return carry

    lax.fori_loop(0, rows // 8, leave, 0)


def row_kernel(half, place, values, table, *refs):
    *outs, held = refs
    tiles, _, both = values.shape
    width = both // 2
    stride = outs[0].shape[0]
    part = table.shape[3] // 2
    whole = stride // part

    def enter_from(offset, first):
        def enter(strip, carry):
            segments = []
            for tile in range(tiles):
                for chunk in range(whole):
                    row = chunk * OVL + strip * 8
                    row = row // half * (2 * half) + lax.rem(row, half) + offset
                    value = values[tile, pl.ds(pl.multiple_of(row, 8), 8), :]
                    segments.append((value[:, :width], value[:, width:]))
            here = pl.ds(pl.multiple_of(first + strip * 8, 8), 8)
            for index, (real, imag) in enumerate(short_fft(segments, -1)):
                held[index, here, :] = real
                held[index, pl.ds(pl.multiple_of(part + first + strip * 8, 8), 8), :] = imag
            return carry

        lax.fori_loop(0, OVL // 8, enter, 0)

    enter_from(half, 0)
    enter_from(0, OVL)

    def multiply(index, carry):
        high, low = split(held[index])
        main = jnp.dot(
            table[0, index], jnp.concatenate([high, low], axis=1), preferred_element_type=F32
        )
        rest = jnp.dot(table[1, index], high, preferred_element_type=F32)
        held[index] = main[:, :width] + (main[:, width:] + rest)
        return carry

    lax.fori_loop(0, tiles * whole, multiply, 0, unroll=UNROLL)

    def leave_as(me):
        def leave(strip, carry):
            here = pl.ds(pl.multiple_of(strip * 8, 8), 8)
            segments = []
            for index in range(tiles * whole):
                below = pl.ds(pl.multiple_of(part + strip * 8, 8), 8)
                segments.append((held[index, here, :], held[index, below, :]))
            for index, (real, imag) in enumerate(short_fft(segments, 1)):
                tile, chunk = index // whole, index % whole
                here = pl.ds(pl.multiple_of(chunk * part + strip * 8, 8), 8)
                outs[tile ^ me][here, pl.ds(0, width)] = real
                outs[tile ^ me][here, pl.ds(width, width)] = imag
            return carry

        @pl.when(place[1] == me)
        def _():
            lax.fori_loop(0, part // 8, leave, 0)

    for me in range(tiles):
        leave_as(me)


def join_kernel(steps, place, *refs):
    blocks, out, done = refs[: len(steps)], refs[-2], refs[-1]
    width = blocks[0].shape[1] // 2
    copies = []
    for step, block in zip(steps, blocks):
        part = jnp.bitwise_xor(place[1], step)
        lanes = pl.ds(pl.multiple_of(part * width, LANES), width)
        for side in range(2):
            copies.append(
                pltpu.make_async_copy(
                    block.at[:, pl.ds(side * width, width)],
                    out.at[side, :, lanes],
                    done.at[len(copies)],
                )
            )
            copies[-1].start()
    for copy in copies:
        copy.wait()


def narrow_join_kernel(place, *refs):
    *blocks, out, ordered = refs
    width = blocks[0].shape[1] // 2
    for step, block in enumerate(blocks):
        ordered[jnp.bitwise_xor(place[1], step)] = block[...]
    for part in range(len(blocks)):
        for side in range(2):
            lanes = pl.ds(part * width, width)
            out[side, :, lanes] = ordered[part, :, pl.ds(side * width, width)]


VMEM = pl.BlockSpec(memory_space=pltpu.VMEM)
SMEM = pl.BlockSpec(memory_space=pltpu.SMEM)
HBM = pl.BlockSpec(memory_space=pltpu.HBM)


def call(kernel, shapes, scratch, limit, micros, *operands, scalars=0, outside=(), to=None):
    return pl.pallas_call(
        kernel,
        out_shape=[jax.ShapeDtypeStruct(shape, F32) for shape in shapes],
        in_specs=[
            SMEM if place < scalars else HBM if place - len(operands) in outside else VMEM
            for place in range(len(operands))
        ],
        out_specs=[to or VMEM] * len(shapes),
        scratch_shapes=scratch,
        cost_estimate=pl.CostEstimate(
            flops=int(micros * 5e8), bytes_accessed=int(micros * 2e6), transcendentals=0
        ),
        compiler_params=pltpu.CompilerParams(vmem_limit_bytes=limit << 20),
    )(*operands)


def local(row_count, col_count, tiles, pupils, intensity, offsets):
    length = tiles.shape[1]
    window = pupils.shape[1]
    leds = intensity.shape[0]
    stride = length - OVL
    whole = stride // LANES
    chunks = whole + 1
    rows = stride // (2 * col_count)
    width = stride // row_count
    fresnel = stride * row_count // 2
    block = (2 * whole + 1, rows, LANES)
    operands = (
        tiles,
        tile_tables(length),
        pupils,
        intensity,
        along_right(right_block(dft_matrix(window))),
        along_left(left_block(dft_matrix(window))),
    )
    buffer = pltpu.VMEM((2, chunks, length, LANES), F32)
    results = [(col_count, *block), (col_count, *block), (OVL // rows, *block)]
    late, early, below = call(
        refine_kernel,
        results,
        [pltpu.VMEM(shape, F32) for shape in results]
        + [pltpu.SemaphoreType.DMA((len(results) * block[0],))]
        + [pltpu.VMEM(operand.shape, operand.dtype) for operand in operands]
        + [
            buffer,
            buffer,
            pltpu.VMEM((leds, 2, window, window), F32),
            pltpu.SemaphoreType.DMA((chunks,)),
            pltpu.SemaphoreType.DMA((len(operands) - 1,)),
        ],
        56,
        22,
        offsets[0, 0],
        *operands,
        scalars=1,
        outside=range(-len(operands), 0),
        to=HBM,
    )
    above = lax.ppermute(below, "row", [(r, (r + 1) % row_count) for r in range(row_count)])
    late = lax.all_to_all(late, "col", split_axis=0, concat_axis=0, tiled=True)
    place = jnp.stack([lax.axis_index("col"), lax.axis_index("row")]).astype(jnp.int32)
    early = call(order_kernel, [block] * col_count, [], 16, 2, place, early, scalars=1)
    *early, token = call(
        spread_kernel, [block] * col_count + [(8, LANES)], [], 16, 40, place, above, *early, scalars=1
    )
    early = [early[0]] + [
        lax.ppermute(early[step], "col", [(c, c ^ step) for c in range(col_count)])
        for step in range(1, col_count)
    ]
    col_classes = col_count * whole
    table = spread_tables(stride * col_count, fresnel, col_classes, lambda m: right_half(m.T))
    scratch = [pltpu.VMEM((col_classes, 2, rows, LANES), F32)]
    (field,) = call(
        after_kernel,
        [(row_count, col_count, rows, 2 * width)],
        scratch,
        32,
        4,
        token,
        late,
        table,
        outside=(-3,),
    )
    (field,) = call(
        gather_kernel,
        [(row_count, col_count, 2 * rows, 2 * width)],
        [pltpu.VMEM((col_count, *block), F32)] + scratch + [pltpu.SemaphoreType.DMA],
        32,
        4,
        place,
        field,
        *early,
        table,
        scalars=1,
    )
    field = field.reshape(row_count * col_count, 2 * rows, 2 * width)
    field = lax.all_to_all(field, ("row", "col"), split_axis=0, concat_axis=0, tiled=True)
    row_classes = row_count * whole
    table = spread_tables(stride * row_count, fresnel, row_classes, left_block)
    shape = (stride, 2 * width)
    blocks = call(
        functools.partial(row_kernel, rows),
        [shape] * row_count,
        [
            pltpu.VMEM((row_classes, 2 * LANES, width), F32),
        ],
        32,
        5,
        place,
        field.reshape(row_count, col_count * 2 * rows, 2 * width),
        table,
        scalars=1,
    )
    blocks = [blocks[0]] + [
        lax.ppermute(blocks[step], "row", [(r, r ^ step) for r in range(row_count)])
        for step in range(1, row_count)
    ]
    whole_shape = (2, stride, stride)
    if width % LANES:
        scratch = [pltpu.VMEM((row_count, *shape), F32)]
        (field,) = call(
            narrow_join_kernel, [whole_shape], scratch, 32, 2, place, *blocks, scalars=1
        )
        return field

    def join(steps, field):
        prior = [] if field is None else [field]
        return pl.pallas_call(
            functools.partial(join_kernel, steps),
            out_shape=jax.ShapeDtypeStruct(whole_shape, F32),
            in_specs=[SMEM] + [VMEM] * len(steps) + [HBM] * len(prior),
            out_specs=HBM,
            scratch_shapes=[pltpu.SemaphoreType.DMA((2 * len(steps),))],
            input_output_aliases={1 + len(steps): 0} if prior else {},
            compiler_params=pltpu.CompilerParams(vmem_limit_bytes=16 << 20),
        )(place, *[blocks[step] for step in steps], *prior)

    return join([row_count - 1], join(range(row_count - 1), None))


def solution(mesh):
    placed = (
        P(None, "row", "col"),
        P(None, "row", "col"),
        P(None, "row", "col"),
        P("row", "col", None, None),
    )
    return jax.shard_map(
        functools.partial(local, mesh.shape["row"], mesh.shape["col"]),
        mesh=mesh,
        in_specs=placed,
        out_specs=P(None, "row", "col"),
        check_vma=False,
    )
```
